256 devices in a mesh: ctx: 128 (over y, z, x), ch: 2 (over core).
Axes of the slice: x: 4, y: 4, z: 8, core: 2. Of those that a mesh axis runs over, the one named last changes fastest.
Arguments:
- query_act: bfloat16 [32768, 512], P('ctx', 'ch'), may hold values from -6 to 6
- key_act: bfloat16 [32768, 512], P('ctx', 'ch'), may hold values from -6 to 6
- value_act: bfloat16 [32768, 512], P('ctx', 'ch'), may hold values from -6 to 6
- filter_taps: float32 [32768, 512], P('ctx', 'ch'), may hold values from -2 to 2
- skip_gain: float32 [512], P('ch'), may hold values from -4 to 4
- out_weight: bfloat16 [512, 512], P('ch'), may hold values from -0.25 to 0.25
- out_grad: bfloat16 [32768, 512], P('ctx', 'ch'), may hold values from -6 to 6
Outputs:
- output: bfloat16 [32768, 512], P('ctx', 'ch')
- grad_query: bfloat16 [32768, 512], P('ctx', 'ch')
- grad_key: bfloat16 [32768, 512], P('ctx', 'ch')
- grad_value: bfloat16 [32768, 512], P('ctx', 'ch')
- grad_filter: float32 [32768, 512], P('ctx', 'ch')
- grad_skip: float32 [512], P('ch')
- grad_out_weight: float32 [512, 512], P('ch')
The draws below stay inside these ranges and needn't reach their ends.
All inputs are finite; a program needn't handle non-finite values.
Results may differ from the reference program's by a relative error of at most 0.0049.
Values may be sent and summed in bfloat16 or wider, within the bound.
A program may use at most 128 MiB of HBM per device.

```python
import math
import jax
import jax.numpy as jnp
from jax import lax

TOKEN_COUNT = 32768
CHANNEL_COUNT = 512


def draw_filter_taps(key, part):
    key = jax.random.fold_in(key, 7)
    falloff_random_key, jitter_random_key, spike_random_key = jax.random.split(key, 3)
    delay_positions = lax.broadcasted_iota(jnp.float32, (TOKEN_COUNT, CHANNEL_COUNT), 0)
    log_rate = jax.random.uniform(falloff_random_key, (1, CHANNEL_COUNT), jnp.float32, math.log(0.5), math.log(TOKEN_COUNT / 40.0))
    jitter_values = jax.random.normal(jitter_random_key, (TOKEN_COUNT, CHANNEL_COUNT), jnp.float32)
    falloff_speed = jnp.exp(log_rate)
    filter_scale = jnp.sqrt((2.0 * falloff_speed + 1.0) / TOKEN_COUNT)
    spike_position = jax.random.randint(spike_random_key, (1, CHANNEL_COUNT), 0, TOKEN_COUNT).astype(jnp.float32)
    spike_amplitude = jnp.where(delay_positions >= spike_position, 0.6, 1.0)
    filter_values = filter_scale * jitter_values * jnp.exp(-falloff_speed * delay_positions / TOKEN_COUNT) * spike_amplitude
    return jnp.clip(filter_values, -2.0, 2.0)


def shard_levels(stream_key, dims, shards, smallest, high):
    def one(position, blocks):
        draws = jax.random.uniform(jax.random.fold_in(jax.random.fold_in(stream_key, 6), position), (blocks,), jnp.float32, smallest / len(shards), high / len(shards))
        return jnp.repeat(jnp.exp(draws), dims[position] // blocks).reshape((-1,) + (1,) * (len(dims) - position - 1))

    factor_of = one(*shards[0])
    for cut in shards[1:]:
        factor_of = factor_of * one(*cut)
    return factor_of


def bell_draw(rng, dims, deviation, most, cuts=(), held_as=jnp.bfloat16):
    level = shard_levels(rng, dims, cuts, -0.22, 0.18) if cuts else 1.0
    array = jax.random.normal(rng, dims, jnp.float32) * deviation * level
    return jnp.minimum(jnp.maximum(array, -most), most).astype(held_as)


def setup_inputs(seed: int = 0) -> dict:
    streams_of = jax.random.split(jax.random.key(seed), 8)
    query_act = bell_draw(streams_of[0], (TOKEN_COUNT, CHANNEL_COUNT), 1.0, 6.0, ((0, 128), (1, 2)))
    key_act = bell_draw(streams_of[1], (TOKEN_COUNT, CHANNEL_COUNT), 1.0, 6.0, ((0, 128), (1, 2)))
    value_act = bell_draw(streams_of[2], (TOKEN_COUNT, CHANNEL_COUNT), 1.0, 6.0, ((0, 128), (1, 2)))
    filter_taps = draw_filter_taps(jax.random.fold_in(streams_of[7], 71), 0)
    skip_gain = bell_draw(streams_of[4], (CHANNEL_COUNT,), 1.0, 4.0, ((0, 2),), jnp.float32)
    out_weight = bell_draw(streams_of[5], (CHANNEL_COUNT, CHANNEL_COUNT), CHANNEL_COUNT ** -0.5, 0.25, ((0, 2),))
    out_grad = bell_draw(streams_of[6], (TOKEN_COUNT, CHANNEL_COUNT), 1.0, 6.0, ((0, 128), (1, 2)))
    return {"query_act": query_act, "key_act": key_act, "value_act": value_act, "filter_taps": filter_taps, "skip_gain": skip_gain, "out_weight": out_weight, "out_grad": out_grad}


def causal(signal, tap_seq):
    total_len = 2 * signal.shape[0]
    sig_spec = jnp.fft.rfft(signal, n=total_len, axis=0)
    tap_spec = jnp.fft.rfft(tap_seq, n=total_len, axis=0)
    return jnp.fft.irfft(sig_spec * tap_spec, n=total_len, axis=0)[:signal.shape[0]]

def correlate(signal, tap_seq):
    total_len = 2 * signal.shape[0]
    sig_spec = jnp.fft.rfft(signal, n=total_len, axis=0)
    tap_spec = jnp.fft.rfft(tap_seq, n=total_len, axis=0)
    return jnp.fft.irfft(sig_spec * jnp.conj(tap_spec), n=total_len, axis=0)[:signal.shape[0]]

def blockwise(block_fn, first, second):
    n_rows, n_chan = first.shape
    group_size = 64 if n_chan % 64 == 0 else n_chan

    def split_cols(array_in):
        return array_in.reshape(n_rows, n_chan // group_size, group_size).transpose(1, 0, 2)
    result = lax.map(lambda block_args: block_fn(block_args[0], block_args[1]), (split_cols(first), split_cols(second)))
    return result.transpose(1, 0, 2).reshape(n_rows, n_chan)

def reference(query_act, key_act, value_act, filter_taps, skip_gain, out_weight, out_grad):
    root_tokens = math.sqrt(TOKEN_COUNT)
    query_f = query_act.astype(jnp.float32)
    key_f = key_act.astype(jnp.float32)
    value_f = value_act.astype(jnp.float32)
    product = key_f * value_f
    conv = blockwise(causal, product, filter_taps)
    mixed_act = conv + skip_gain * product
    gated_act = (query_f * mixed_act).astype(jnp.bfloat16)
    output = jnp.dot(gated_act, out_weight, preferred_element_type=jnp.float32).astype(jnp.bfloat16)
    d_gated = jnp.dot(out_grad, out_weight.T, preferred_element_type=jnp.float32)
    grad_query = (d_gated * mixed_act).astype(jnp.bfloat16)
    d_mixed = d_gated * query_f
    grad_product = blockwise(correlate, d_mixed, filter_taps) + skip_gain * d_mixed
    grad_filter = blockwise(correlate, d_mixed, product) / root_tokens
    grad_skip = lax.optimization_barrier(jnp.sum(d_mixed * product, axis=0)) / root_tokens
    grad_key = (grad_product * value_f).astype(jnp.bfloat16)
    grad_value = (grad_product * key_f).astype(jnp.bfloat16)
    grad_out_weight = jnp.dot(gated_act.T, out_grad, preferred_element_type=jnp.float32) / root_tokens
    return (output, grad_query, grad_key, grad_value, grad_filter, grad_skip, grad_out_weight)
```

```python
import math

import jax
import jax.numpy as jnp
import numpy as np
import ml_dtypes
from jax import lax
from jax.experimental import pallas as pl
from jax.experimental.pallas import tpu as pltpu
from jax.sharding import PartitionSpec as P

MESH = pl.DeviceIdType.MESH
F32, BF16 = jnp.float32, jnp.bfloat16
NCTX = 128
NY, NZ, NX = 4, 8, 4
LEN = 32768
ROOT = math.sqrt(LEN)


def split_table(table):
    table = table.astype(np.float32)
    hi = table.astype(ml_dtypes.bfloat16)
    lo = (table - hi.astype(np.float32)).astype(ml_dtypes.bfloat16)
    return hi, lo


def tables():
    n1 = np.arange(128)
    n2 = np.arange(256)
    ang = -2 * np.pi * ((n1[None, :] * (4 * n1[:, None] + 1)) % 512) / 512
    a_hi, a_lo = split_table(np.concatenate([np.cos(ang), np.sin(ang)], 0))
    a_cat = np.concatenate([a_hi, a_lo], 1)
    c_hi, c_lo = split_table(np.concatenate([np.cos(ang.T), np.sin(ang.T)], 1) / LEN)
    c_cat = np.concatenate([c_hi, c_lo, c_hi], 1)
    tw = -2 * np.pi * ((n2[None, :] * (4 * n1[:, None] + 1)) % (4 * LEN)) / (4 * LEN)
    t_re, t_im = np.cos(tw).astype(np.float32), np.sin(tw).astype(np.float32)
    bang = -2 * np.pi * ((n2[:, None] * n2[None, :]) % 256) / 256
    b_hi, b_lo = split_table(np.concatenate([np.cos(bang), np.sin(bang)], 1))
    b_cat = np.concatenate([b_hi, b_lo, b_hi], 0)
    return a_cat, b_cat, c_cat, t_re, t_im


def dot(a, b, dims=(((1,), (0,)), ((), ()))):
    return lax.dot_general(a, b, dims, preferred_element_type=F32)


def split(val):
    hi = val.astype(BF16)
    return hi, (val - hi.astype(F32)).astype(BF16)


def kernel(
    q_ref, k_ref, v_ref, taps_ref, skip_ref, w_ref, g_ref, a_ref, b_ref, c_ref, tr_ref, ti_ref,
    out_ref, gq_ref, gk_ref, gv_ref, gf_ref, gs_ref, gw_ref,
    s1, r1, s2, r2, s3, r3, s4, r4,
    i8, i4, prod, dmix, dgat, gfull, gboth, w_oth, gat_oth,
    sig_re, sig_im, tap_re, tap_im,
    g1, rg, sz, rz, az, ga, sk, rsk1, sk2, rsk2,
    lsem, ssem, rsem,
):
    me = lax.axis_index("ctx")
    ch = lax.axis_index("ch")
    y, z, x = me // 32, lax.rem(me // 4, NZ), lax.rem(me, NX)
    plane = y * NX + x

    def peer(idx):
        return {"ctx": idx}

    def remote(src, dst, sem, device):
        return pltpu.make_async_remote_copy(
            src_ref=src, dst_ref=dst, send_sem=ssem.at[sem], recv_sem=rsem.at[sem],
            device_id=device, device_id_type=MESH,
        )

    def at_plane(idx):
        return peer(idx // NX * 32 + z * NX + lax.rem(idx, NX))

    def at_z(idx):
        return peer(y * 32 + idx * NX + x)

    sibling = {"ch": 1 - ch}

    bar = pltpu.get_barrier_semaphore()

    def greet(step, carry):
        pl.semaphore_signal(bar, inc=1, device_id=peer(lax.rem(me + step, NCTX)), device_id_type=MESH)
        return carry

    lax.fori_loop(1, NCTX, greet, 0)
    pl.semaphore_signal(bar, inc=1, device_id=sibling, device_id_type=MESH)

    def interleave(blocks, tmp, dst):
        rows = len(blocks)
        for r, blk in enumerate(blocks):
            tmp[pl.ds(r, 128, stride=rows), :] = blk
        dst[...] = tmp[...].reshape(128, rows, 128).astype(BF16)

    def separate(src, tmp, rows):
        tmp[...] = src[...].astype(F32).reshape(128 * rows, 128)
        return [tmp[pl.ds(r, 128, stride=rows), :] for r in range(rows)]

    def send_all(src, dst, sem, lslot):
        pltpu.make_async_copy(src.at[me], dst.at[me], lsem.at[lslot]).start()

        def go(step, carry):
            to = lax.rem(me + step, NCTX)
            remote(src.at[to], dst.at[me], sem, peer(to)).start()
            return carry

        lax.fori_loop(1, NCTX, go, 0)

    def wait_all(src, dst, sem, lslot):
        pltpu.make_async_copy(src.at[me], dst.at[me], lsem.at[lslot]).wait()
        whole = remote(
            src.at[pl.ds(0, NCTX - 1)], dst.at[pl.ds(0, NCTX - 1)], sem, peer(lax.rem(me + 1, NCTX))
        )
        whole.wait_recv()
        whole.wait_send()

    def blocks_of(val):
        return [
            val[th * 128:(th + 1) * 128, h * 128:(h + 1) * 128].T for h in range(2) for th in range(2)
        ]

    def tokens_of(blks):
        return jnp.concatenate(
            [jnp.concatenate([blks[th].T, blks[2 + th].T], 1) for th in range(2)], 0
        )

    def forward(blks):
        sig = jnp.concatenate(blks, 1).astype(BF16)
        spec = dot(a_ref[...], jnp.concatenate([sig, sig], 0))
        re, im = spec[:128], spec[128:]
        t_re, t_im = tr_ref[...], ti_ref[...]
        top, bottom = [], []
        for h in range(2):
            u, w = re[:, h * 256:(h + 1) * 256], im[:, h * 256:(h + 1) * 256]
            top.append(u * t_re - w * t_im)
            bottom.append(u * t_im + w * t_re)
        hi, lo = split(jnp.concatenate(top + bottom, 0))
        full = dot(jnp.concatenate([hi, hi, lo], 1), b_ref[...])
        return full[:256, :256] - full[256:, 256:], full[:256, 256:] + full[256:, :256]

    def inverse(re, im):
        hi, lo = split(jnp.concatenate([re, im], 0))
        full = dot(jnp.concatenate([hi, hi, lo], 1), b_ref[...])
        u = full[:256, :256] + full[256:, 256:]
        w = full[256:, :256] - full[:256, 256:]
        t_re, t_im = tr_ref[...], ti_ref[...]
        top, bottom = [], []
        for h in range(2):
            ur, wi = u[h * 128:(h + 1) * 128], w[h * 128:(h + 1) * 128]
            top.append(ur * t_re + wi * t_im)
            bottom.append(wi * t_re - ur * t_im)
        both = jnp.concatenate([jnp.concatenate(top, 1), jnp.concatenate(bottom, 1)], 0)
        hi, lo = split(both)
        sig = dot(c_ref[...], jnp.concatenate([hi, hi, lo], 0))
        return [sig[:, r * 128:(r + 1) * 128] for r in range(4)]

    prod[...] = k_ref[...].astype(F32) * v_ref[...].astype(F32)
    interleave(blocks_of(prod[...]) + blocks_of(taps_ref[...]), i8, s1)
    pl.semaphore_wait(bar, NCTX)
    g_send = remote(g_ref, gboth, 8, sibling)
    g_send.start()
    w_send = remote(w_ref.at[:, pl.ds(pl.multiple_of((1 - ch) * 256, 256), 256)], w_oth, 9, sibling)
    w_send.start()
    send_all(s1, r1, 0, 0)

    g_send.wait()
    mine, other = g_ref[...], gboth[...]
    first = ch == 0
    gfull[:, :256] = jnp.where(first, mine.astype(F32), other.astype(F32)).astype(BF16)
    gfull[:, 256:] = jnp.where(first, other.astype(F32), mine.astype(F32)).astype(BF16)
    dgat[...] = dot(gfull[...], w_ref[...], (((1,), (1,)), ((), ())))
    dmix[...] = dgat[...] * q_ref[...].astype(F32)
    interleave(blocks_of(dmix[...]), i4, s2)
    send_all(s2, r2, 1, 1)

    sk[...] = jnp.broadcast_to(jnp.sum(dmix[...] * prod[...], axis=0, keepdims=True), (8, 256))
    for step in range(1, 16):
        remote(sk, rsk1.at[plane], 4, at_plane(lax.rem(plane + step, 16))).start()

    wait_all(s1, r1, 0, 0)
    blks = separate(r1, i8, 8)
    re, im = forward(blks[:4])
    sig_re[...], sig_im[...] = re, im
    re, im = forward(blks[4:])
    tap_re[...], tap_im[...] = re, im
    re, im = sig_re[...], sig_im[...]
    conv = inverse(re * tap_re[...] - im * tap_im[...], re * tap_im[...] + im * tap_re[...])
    interleave(conv, i4, s3)
    send_all(s3, r3, 2, 2)

    wsk = remote(rsk1.at[pl.ds(0, 15)], rsk1.at[pl.ds(0, 15)], 4, at_plane(lax.rem(plane + 1, 16)))
    wsk.wait_recv()
    wsk.wait_send()
    rsk1[plane] = sk[...]
    sk2[...] = jnp.sum(rsk1[...], axis=0)
    for step in range(1, NZ):
        remote(sk2, rsk2.at[z], 5, at_z(lax.rem(z + step, NZ))).start()

    wait_all(s2, r2, 1, 1)
    re, im = forward(separate(r2, i4, 4))
    lag_p = inverse(re * tap_re[...] + im * tap_im[...], im * tap_re[...] - re * tap_im[...])
    lag_f = inverse(re * sig_re[...] + im * sig_im[...], im * sig_re[...] - re * sig_im[...])
    interleave(lag_p + lag_f, i8, s4)
    send_all(s4, r4, 3, 3)

    wait_all(s3, r3, 2, 2)
    skip = skip_ref[...]
    mixed = tokens_of(separate(r3, i4, 4)) + skip * prod[...]
    gated = (q_ref[...].astype(F32) * mixed).astype(BF16)
    gq_ref[...] = (dgat[...] * mixed).astype(BF16)
    g1[...] = dot(gated, gfull[...], (((0,), (0,)), ((), ()))).astype(BF16)
    for step in range(1, 16):
        to = lax.rem(plane + step, 16)
        remote(
            g1.at[pl.ds(pl.multiple_of(to * 16, 16), 16)], rg.at[plane], 6, at_plane(to)
        ).start()
    s_gat = gat_oth.at[0]
    gat_oth[0] = gated
    gat_send = remote(s_gat, gat_oth.at[1], 10, sibling)
    gat_send.start()
    w_send.wait()
    w_mine = w_ref[:, pl.ds(pl.multiple_of(ch * 256, 256), 256)]
    part = dot(gated, w_mine)
    gat_send.wait()
    out_ref[...] = (part + dot(gat_oth[1], w_oth[...])).astype(BF16)

    wrg = remote(rg.at[pl.ds(0, 15)], rg.at[pl.ds(0, 15)], 6, at_plane(lax.rem(plane + 1, 16)))
    wrg.wait_recv()
    wrg.wait_send()
    rg[plane] = g1[pl.ds(pl.multiple_of(plane * 16, 16), 16), :]
    total = jnp.sum(rg[...].astype(F32), axis=0)
    for i in range(NZ):
        sz[i] = total[i // 4 * 8:i // 4 * 8 + 8, i % 4 * 128:i % 4 * 128 + 128]
    for step in range(1, NZ):
        to = lax.rem(z + step, NZ)
        remote(sz.at[to], rz.at[z], 7, at_z(to)).start()
    wsk = remote(rsk2.at[pl.ds(0, 7)], rsk2.at[pl.ds(0, 7)], 5, at_z(lax.rem(z + 1, NZ)))
    wsk.wait_recv()
    wsk.wait_send()
    rsk2[z] = sk2[...]
    gs_ref[...] = jnp.sum(rsk2[...], axis=0) / ROOT
    wrz = remote(rz.at[pl.ds(0, 7)], rz.at[pl.ds(0, 7)], 7, at_z(lax.rem(z + 1, NZ)))
    wrz.wait_recv()
    wrz.wait_send()
    rz[z] = sz[z]
    az[z] = jnp.sum(rz[...], axis=0) / ROOT
    for step in range(1, NZ):
        remote(az.at[z], az.at[z], 11, at_z(lax.rem(z + step, NZ))).start()
    waz = remote(az.at[pl.ds(0, 7)], az.at[pl.ds(0, 7)], 11, at_z(lax.rem(z + 1, NZ)))
    waz.wait_recv()
    waz.wait_send()
    rows = [jnp.concatenate([az[4 * i + j] for j in range(4)], 1) for i in range(2)]
    ga[plane] = jnp.concatenate(rows, 0).astype(BF16)
    for step in range(1, 16):
        remote(ga.at[plane], ga.at[plane], 12, at_plane(lax.rem(plane + step, 16))).start()

    wait_all(s4, r4, 3, 3)
    blks = separate(r4, i8, 8)
    grad_prod = tokens_of(blks[:4]) + skip * dmix[...]
    gk_ref[...] = (grad_prod * v_ref[...].astype(F32)).astype(BF16)
    gv_ref[...] = (grad_prod * k_ref[...].astype(F32)).astype(BF16)
    gf_ref[...] = tokens_of(blks[4:]) / ROOT

    wga = remote(ga.at[pl.ds(0, 15)], ga.at[pl.ds(0, 15)], 12, at_plane(lax.rem(plane + 1, 16)))
    wga.wait_recv()
    wga.wait_send()
    gw_ref[...] = ga[...].astype(F32).reshape(256, 512)


def shards(query_act, key_act, value_act, filter_taps, skip_gain, out_weight, out_grad):
    a_cat, b_cat, c_cat, t_re, t_im = (jnp.asarray(t) for t in tables())
    vmem = pl.BlockSpec(memory_space=pltpu.VMEM)
    sds = jax.ShapeDtypeStruct
    outs = pl.pallas_call(
        kernel,
        out_shape=(
            sds((256, 256), BF16), sds((256, 256), BF16), sds((256, 256), BF16),
            sds((256, 256), BF16), sds((256, 256), F32), sds((8, 256), F32), sds((256, 512), F32),
        ),
        in_specs=[vmem] * 12,
        out_specs=[vmem] * 7,
        scratch_shapes=[
            pltpu.VMEM((128, 8, 128), BF16), pltpu.VMEM((128, 8, 128), BF16),
            pltpu.VMEM((128, 4, 128), BF16), pltpu.VMEM((128, 4, 128), BF16),
            pltpu.VMEM((128, 4, 128), BF16), pltpu.VMEM((128, 4, 128), BF16),
            pltpu.VMEM((128, 8, 128), BF16), pltpu.VMEM((128, 8, 128), BF16),
            pltpu.VMEM((1024, 128), F32), pltpu.VMEM((512, 128), F32),
            pltpu.VMEM((256, 256), F32), pltpu.VMEM((256, 256), F32), pltpu.VMEM((256, 256), F32),
            pltpu.VMEM((256, 512), BF16), pltpu.VMEM((256, 256), BF16),
            pltpu.VMEM((256, 256), BF16), pltpu.VMEM((2, 256, 256), BF16),
            pltpu.VMEM((256, 256), F32), pltpu.VMEM((256, 256), F32),
            pltpu.VMEM((256, 256), F32), pltpu.VMEM((256, 256), F32),
            pltpu.VMEM((256, 512), BF16), pltpu.VMEM((16, 16, 512), BF16),
            pltpu.VMEM((8, 8, 128), F32), pltpu.VMEM((8, 8, 128), F32), pltpu.VMEM((8, 8, 128), F32),
            pltpu.VMEM((16, 16, 512), BF16),
            pltpu.VMEM((8, 256), F32), pltpu.VMEM((16, 8, 256), F32),
            pltpu.VMEM((8, 256), F32), pltpu.VMEM((8, 8, 256), F32),
            pltpu.SemaphoreType.DMA((4,)), pltpu.SemaphoreType.DMA((13,)), pltpu.SemaphoreType.DMA((13,)),
        ],
        compiler_params=pltpu.CompilerParams(
            collective_id=0, has_side_effects=True, vmem_limit_bytes=48 * 1024 * 1024
        ),
        name="hyena",
    )(
        query_act, key_act, value_act, filter_taps, skip_gain[None, :], out_weight, out_grad,
        a_cat, b_cat, c_cat, t_re, t_im,
    )
    out, gq, gk, gv, gf, gs, gw = outs
    return out, gq, gk, gv, gf, gs[0], gw


def solution(mesh):
    spec = P("ctx", "ch")
    in_specs = (spec, spec, spec, spec, P("ch"), P("ch", None), spec)
    out_specs = (spec, spec, spec, spec, spec, P("ch"), P("ch", None))
    return jax.shard_map(shards, mesh=mesh, in_specs=in_specs, out_specs=out_specs, check_vma=False)
```

```python
import math

import jax
import jax.numpy as jnp
import numpy as np
import ml_dtypes
from jax import lax
from jax.experimental import pallas as pl
from jax.experimental.pallas import tpu as pltpu
from jax.sharding import PartitionSpec as P

MESH = pl.DeviceIdType.MESH
F32, BF16 = jnp.float32, jnp.bfloat16
NCTX = 128
NY, NZ, NX = 4, 8, 4
LEN = 32768
ROOT = math.sqrt(LEN)


def split_table(table):
    table = table.astype(np.float32)
    hi = table.astype(ml_dtypes.bfloat16)
    lo = (table - hi.astype(np.float32)).astype(ml_dtypes.bfloat16)
    return hi, lo


def tables():
    n1 = np.arange(128)
    n2 = np.arange(256)
    ang = -2 * np.pi * ((n1[None, :] * (4 * n1[:, None] + 1)) % 512) / 512
    a_hi, a_lo = split_table(np.concatenate([np.cos(ang), np.sin(ang)], 0))
    a_cat = np.concatenate([a_hi, a_lo], 1)
    c_hi, c_lo = split_table(np.concatenate([np.cos(ang.T), np.sin(ang.T)], 1) / LEN)
    c_cat = np.concatenate([c_hi, c_lo, c_hi], 1)
    tw = -2 * np.pi * ((n2[None, :] * (4 * n1[:, None] + 1)) % (4 * LEN)) / (4 * LEN)
    t_re, t_im = np.cos(tw).astype(np.float32), np.sin(tw).astype(np.float32)
    bang = -2 * np.pi * ((n2[:, None] * n2[None, :]) % 256) / 256
    b_hi, b_lo = split_table(np.concatenate([np.cos(bang), np.sin(bang)], 1))
    b_cat = np.concatenate([b_hi, b_lo, b_hi], 0)
    return a_cat, b_cat, c_cat, t_re, t_im


def dot(a, b, dims=(((1,), (0,)), ((), ()))):
    return lax.dot_general(a, b, dims, preferred_element_type=F32)


def split(val):
    hi = val.astype(BF16)
    return hi, (val - hi.astype(F32)).astype(BF16)


ORDER4 = (2, 1, 3, 0)
ORDER8 = (4, 3, 5, 2, 6, 1, 7, 0)


def kernel(
    q_hbm, k_hbm, v_hbm, taps_hbm, skip_hbm, w_hbm, g_hbm, a_hbm, b_hbm, c_hbm, tr_hbm, ti_hbm,
    out_ref, gq_ref, gk_ref, gv_ref, gf_ref, gs_ref, gw_ref,
    q_ref, k_ref, v_ref, taps_ref, skip_ref, w_ref, g_ref, a_ref, b_ref, c_ref, tr_ref, ti_ref,
    s0, r0, s1, r1, s2, r2, s3, r3, s4, r4,
    i8, i4, prod, dmix, dgat, gfull, gboth, w_oth, gat_oth,
    sig_re, sig_im, tap_re, tap_im,
    g1, rg, sz, rz, az, ga, sk, rsk1, sk2, rsk2,
    isem, lsem, ssem, rsem,
):
    me = lax.axis_index("ctx")
    ch = lax.axis_index("ch")
    y, z, x = me // 32, lax.rem(me // 4, NZ), lax.rem(me, NX)
    plane = y * NX + x

    loads = {}
    pairs = (
        (k_hbm, k_ref), (v_hbm, v_ref), (taps_hbm, taps_ref), (g_hbm, g_ref), (w_hbm, w_ref),
        (q_hbm, q_ref), (a_hbm, a_ref), (tr_hbm, tr_ref), (ti_hbm, ti_ref), (b_hbm, b_ref),
        (c_hbm, c_ref), (skip_hbm, skip_ref),
    )
    for i, (src, dst) in enumerate(pairs):
        loads[i] = pltpu.make_async_copy(src, dst, isem.at[i])
        loads[i].start()

    def peer(idx):
        return {"ctx": idx}

    def remote(src, dst, sem, device):
        return pltpu.make_async_remote_copy(
            src_ref=src, dst_ref=dst, send_sem=ssem.at[sem], recv_sem=rsem.at[sem],
            device_id=device, device_id_type=MESH,
        )

    def at_plane(idx):
        return peer(idx // NX * 32 + z * NX + lax.rem(idx, NX))

    def at_z(idx):
        return peer(y * 32 + idx * NX + x)

    plane_order = [
        lax.rem(y + dy, NY) * NX + lax.rem(x + dx, NX) for dy in ORDER4 for dx in ORDER4
    ][:15]
    z_order = [lax.rem(z + dz, NZ) for dz in ORDER8][:7]
    sibling = {"ch": 1 - ch}

    bar = pltpu.get_barrier_semaphore()

    def greet(step, carry):
        pl.semaphore_signal(bar, inc=1, device_id=peer(lax.rem(me + 1 + step, NCTX)), device_id_type=MESH)
        return carry

    lax.fori_loop(0, NCTX - 1, greet, 0)
    pl.semaphore_signal(bar, inc=1, device_id=sibling, device_id_type=MESH)

    def interleave(blocks, tmp, dst):
        rows = len(blocks)
        for r, blk in enumerate(blocks):
            tmp[pl.ds(r, 128, stride=rows), :] = blk
        dst[...] = tmp[...].reshape(128, rows, 128).astype(BF16)

    def separate(src, tmp, rows):
        tmp[...] = src[...].astype(F32).reshape(128 * rows, 128)
        return [tmp[pl.ds(r, 128, stride=rows), :] for r in range(rows)]

    def send_all(src, dst, sem):
        pltpu.make_async_copy(src.at[me], dst.at[me], lsem.at[sem]).start()

        def go(step, carry):
            to = lax.rem(me + 1 + step, NCTX)
            remote(src.at[to], dst.at[me], sem, peer(to)).start()
            return carry

        lax.fori_loop(0, NCTX - 1, go, 0)

    def whole(src, dst, sem):
        return remote(
            src.at[pl.ds(0, NCTX - 1)], dst.at[pl.ds(0, NCTX - 1)], sem, peer(lax.rem(me + 1, NCTX))
        )

    def wait_all(src, dst, sem):
        pltpu.make_async_copy(src.at[me], dst.at[me], lsem.at[sem]).wait()
        whole(src, dst, sem).wait_recv()

    def some(buf, count, sem, device):
        part = buf.at[pl.ds(0, count)]
        return remote(part, part, sem, device)

    def blocks_of(val):
        return [
            val[th * 128:(th + 1) * 128, h * 128:(h + 1) * 128].T for h in range(2) for th in range(2)
        ]

    def tokens_of(blks):
        return jnp.concatenate(
            [jnp.concatenate([blks[th].T, blks[2 + th].T], 1) for th in range(2)], 0
        )

    def forward(blks):
        sig = jnp.concatenate(blks, 1).astype(BF16)
        spec = dot(a_ref[...], jnp.concatenate([sig, sig], 0))
        re, im = spec[:128], spec[128:]
        t_re, t_im = tr_ref[...], ti_ref[...]
        top, bottom = [], []
        for h in range(2):
            u, w = re[:, h * 256:(h + 1) * 256], im[:, h * 256:(h + 1) * 256]
            top.append(u * t_re - w * t_im)
            bottom.append(u * t_im + w * t_re)
        hi, lo = split(jnp.concatenate(top + bottom, 0))
        full = dot(jnp.concatenate([hi, hi, lo], 1), b_ref[...])
        return full[:256, :256] - full[256:, 256:], full[:256, 256:] + full[256:, :256]

    def inverse(re, im):
        hi, lo = split(jnp.concatenate([re, im], 0))
        full = dot(jnp.concatenate([hi, hi, lo], 1), b_ref[...])
        u = full[:256, :256] + full[256:, 256:]
        w = full[256:, :256] - full[:256, 256:]
        t_re, t_im = tr_ref[...], ti_ref[...]
        top, bottom = [], []
        for h in range(2):
            ur, wi = u[h * 128:(h + 1) * 128], w[h * 128:(h + 1) * 128]
            top.append(ur * t_re + wi * t_im)
            bottom.append(wi * t_re - ur * t_im)
        both = jnp.concatenate([jnp.concatenate(top, 1), jnp.concatenate(bottom, 1)], 0)
        hi, lo = split(both)
        sig = dot(c_ref[...], jnp.concatenate([hi, hi, lo], 0))
        return [sig[:, r * 128:(r + 1) * 128] for r in range(4)]

    loads[0].wait()
    loads[1].wait()
    prod[...] = k_ref[...].astype(F32) * v_ref[...].astype(F32)
    interleave(blocks_of(prod[...]), i4, s0)
    loads[2].wait()
    interleave(blocks_of(taps_ref[...]), i4, s1)
    loads[3].wait()
    loads[4].wait()
    pl.semaphore_wait(bar, NCTX)
    g_send = remote(g_ref, gboth, 9, sibling)
    g_send.start()
    w_send = remote(w_ref.at[:, pl.ds(pl.multiple_of((1 - ch) * 256, 256), 256)], w_oth, 10, sibling)
    w_send.start()
    send_all(s0, r0, 0)
    send_all(s1, r1, 1)

    loads[5].wait()
    g_send.wait_recv()
    mine, other = g_ref[...], gboth[...]
    first = ch == 0
    gfull[:, :256] = jnp.where(first, mine.astype(F32), other.astype(F32)).astype(BF16)
    gfull[:, 256:] = jnp.where(first, other.astype(F32), mine.astype(F32)).astype(BF16)
    dgat[...] = dot(gfull[...], w_ref[...], (((1,), (1,)), ((), ())))
    dmix[...] = dgat[...] * q_ref[...].astype(F32)
    interleave(blocks_of(dmix[...]), i4, s2)
    send_all(s2, r2, 2)

    sk[...] = jnp.broadcast_to(jnp.sum(dmix[...] * prod[...], axis=0, keepdims=True), (8, 256))
    for to in plane_order:
        remote(sk, rsk1.at[plane], 5, at_plane(to)).start()
    for i in range(6, 12):
        loads[i].wait()

    wait_all(s0, r0, 0)
    re, im = forward(separate(r0, i4, 4))
    sig_re[...], sig_im[...] = re, im
    wait_all(s1, r1, 1)
    re, im = forward(separate(r1, i4, 4))
    tap_re[...], tap_im[...] = re, im
    re, im = sig_re[...], sig_im[...]
    conv = inverse(re * tap_re[...] - im * tap_im[...], re * tap_im[...] + im * tap_re[...])
    interleave(conv, i4, s3)
    send_all(s3, r3, 3)

    some(rsk1, 15, 5, at_plane(plane_order[0])).wait_recv()
    rsk1[plane] = sk[...]
    sk2[...] = jnp.sum(rsk1[...], axis=0)
    for to in z_order:
        remote(sk2, rsk2.at[z], 6, at_z(to)).start()

    wait_all(s2, r2, 2)
    re, im = forward(separate(r2, i4, 4))
    lag_p = inverse(re * tap_re[...] + im * tap_im[...], im * tap_re[...] - re * tap_im[...])
    lag_f = inverse(re * sig_re[...] + im * sig_im[...], im * sig_re[...] - re * sig_im[...])
    interleave(lag_p + lag_f, i8, s4)
    send_all(s4, r4, 4)

    wait_all(s3, r3, 3)
    skip = skip_ref[...]
    mixed = tokens_of(separate(r3, i4, 4)) + skip * prod[...]
    gated = (q_ref[...].astype(F32) * mixed).astype(BF16)
    g1[...] = dot(gated, gfull[...], (((0,), (0,)), ((), ()))).astype(BF16)
    for to in plane_order:
        remote(
            g1.at[pl.ds(pl.multiple_of(to * 16, 16), 16)], rg.at[plane], 7, at_plane(to)
        ).start()
    gat_oth[0] = gated
    gat_send = remote(gat_oth.at[0], gat_oth.at[1], 11, sibling)
    gat_send.start()
    gq_ref[...] = (dgat[...] * mixed).astype(BF16)
    w_send.wait_recv()
    w_mine = w_ref[:, pl.ds(pl.multiple_of(ch * 256, 256), 256)]
    part = dot(gated, w_mine)
    gat_send.wait_recv()
    out_ref[...] = (part + dot(gat_oth[1], w_oth[...])).astype(BF16)

    some(rg, 15, 7, at_plane(plane_order[0])).wait_recv()
    rg[plane] = g1[pl.ds(pl.multiple_of(plane * 16, 16), 16), :]
    total = jnp.sum(rg[...].astype(F32), axis=0)
    for i in range(NZ):
        sz[i] = total[i // 4 * 8:i // 4 * 8 + 8, i % 4 * 128:i % 4 * 128 + 128]
    for to in z_order:
        remote(sz.at[to], rz.at[z], 8, at_z(to)).start()
    some(rsk2, 7, 6, at_z(z_order[0])).wait_recv()
    rsk2[z] = sk2[...]
    gs_ref[...] = jnp.sum(rsk2[...], axis=0)[:1] / ROOT
    some(rz, 7, 8, at_z(z_order[0])).wait_recv()
    rz[z] = sz[z]
    az[z] = jnp.sum(rz[...], axis=0) / ROOT
    for to in z_order:
        remote(az.at[z], az.at[z], 12, at_z(to)).start()
    some(az, 7, 12, at_z(z_order[0])).wait_recv()
    rows = [jnp.concatenate([az[4 * i + j] for j in range(4)], 1) for i in range(2)]
    ga[plane] = jnp.concatenate(rows, 0).astype(BF16)
    for to in plane_order:
        remote(ga.at[plane], ga.at[plane], 13, at_plane(to)).start()

    wait_all(s4, r4, 4)
    blks = separate(r4, i8, 8)
    grad_prod = tokens_of(blks[:4]) + skip * dmix[...]
    gk_ref[...] = (grad_prod * v_ref[...].astype(F32)).astype(BF16)
    gv_ref[...] = (grad_prod * k_ref[...].astype(F32)).astype(BF16)
    gf_ref[...] = tokens_of(blks[4:]) / ROOT

    whole(s0, r0, 0).wait_send()
    whole(s1, r1, 1).wait_send()
    whole(s2, r2, 2).wait_send()
    whole(s3, r3, 3).wait_send()
    whole(s4, r4, 4).wait_send()
    some(rsk1, 15, 5, at_plane(plane_order[0])).wait_send()
    some(rsk2, 7, 6, at_z(z_order[0])).wait_send()
    some(rg, 15, 7, at_plane(plane_order[0])).wait_send()
    some(rz, 7, 8, at_z(z_order[0])).wait_send()
    g_send.wait_send()
    w_send.wait_send()
    gat_send.wait_send()
    some(az, 7, 12, at_z(z_order[0])).wait_send()

    last = some(ga, 15, 13, at_plane(plane_order[0]))
    last.wait_recv()
    gw_ref[...] = ga[...].astype(F32).reshape(256, 512)
    last.wait_send()


def finish(*refs):
    count = len(refs) // 2
    for src, dst in zip(refs[:count], refs[count:]):
        dst[...] = src[...]


def shards(query_act, key_act, value_act, filter_taps, skip_gain, out_weight, out_grad):
    a_cat, b_cat, c_cat, t_re, t_im = (jnp.asarray(t) for t in tables())
    vmem = pl.BlockSpec(memory_space=pltpu.VMEM)
    anywhere = pl.BlockSpec(memory_space=pl.ANY)
    sds = jax.ShapeDtypeStruct
    operands = (
        query_act, key_act, value_act, filter_taps, skip_gain[None, :], out_weight, out_grad,
        a_cat, b_cat, c_cat, t_re, t_im,
    )
    results = (
        sds((256, 256), BF16), sds((256, 256), BF16), sds((256, 256), BF16),
        sds((256, 256), BF16), sds((256, 256), F32), sds((1, 256), F32), sds((256, 512), F32),
    )
    msg4, msg8 = pltpu.VMEM((128, 4, 128), BF16), pltpu.VMEM((128, 8, 128), BF16)
    square, half = pltpu.VMEM((256, 256), F32), pltpu.VMEM((256, 256), BF16)
    outs = pl.pallas_call(
        kernel,
        out_shape=results,
        in_specs=[anywhere] * 12,
        out_specs=[vmem] * 7,
        scratch_shapes=[pltpu.VMEM(op.shape, op.dtype) for op in operands] + [
            msg4, msg4, msg4, msg4, msg4, msg4, msg4, msg4, msg8, msg8,
            pltpu.VMEM((1024, 128), F32), pltpu.VMEM((512, 128), F32),
            square, square, square,
            pltpu.VMEM((256, 512), BF16), half, half, pltpu.VMEM((2, 256, 256), BF16),
            square, square, square, square,
            pltpu.VMEM((256, 512), BF16), pltpu.VMEM((16, 16, 512), BF16),
            pltpu.VMEM((8, 8, 128), F32), pltpu.VMEM((8, 8, 128), F32), pltpu.VMEM((8, 8, 128), F32),
            pltpu.VMEM((16, 16, 512), BF16),
            pltpu.VMEM((8, 256), F32), pltpu.VMEM((16, 8, 256), F32),
            pltpu.VMEM((8, 256), F32), pltpu.VMEM((8, 8, 256), F32),
            pltpu.SemaphoreType.DMA((12,)), pltpu.SemaphoreType.DMA((5,)),
            pltpu.SemaphoreType.DMA((14,)), pltpu.SemaphoreType.DMA((14,)),
        ],
        compiler_params=pltpu.CompilerParams(
            collective_id=0, has_side_effects=True, vmem_limit_bytes=56 * 1024 * 1024
        ),
        name="hyena",
    )(*operands)
    outs = pl.pallas_call(
        finish,
        out_shape=results,
        in_specs=[vmem] * 7,
        out_specs=[vmem] * 7,
        name="finish",
    )(*outs)
    out, gq, gk, gv, gf, gs, gw = outs
    return out, gq, gk, gv, gf, gs.reshape(256), gw


def solution(mesh):
    spec = P("ctx", "ch")
    in_specs = (spec, spec, spec, spec, P("ch"), P("ch", None), spec)
    out_specs = (spec, spec, spec, spec, spec, P("ch"), P("ch", None))
    return jax.shard_map(shards, mesh=mesh, in_specs=in_specs, out_specs=out_specs, check_vma=False)
```

```python
import math

import jax
import jax.numpy as jnp
import numpy as np
import ml_dtypes
from jax import lax
from jax.experimental import pallas as pl
from jax.experimental.pallas import tpu as pltpu
from jax.sharding import PartitionSpec as P

MESH = pl.DeviceIdType.MESH
F32, BF16 = jnp.float32, jnp.bfloat16
NCTX = 128
NY, NZ, NX = 4, 8, 4
LEN = 32768
ROOT = math.sqrt(LEN)
LAG_CUTS = (40, 84)


def split_table(table):
    table = table.astype(np.float32)
    hi = table.astype(ml_dtypes.bfloat16)
    lo = (table - hi.astype(np.float32)).astype(ml_dtypes.bfloat16)
    return hi, lo


def tables():
    n1 = np.arange(128)
    n2 = np.arange(256)
    ang = -2 * np.pi * ((n1[None, :] * (4 * n1[:, None] + 1)) % 512) / 512
    a_hi, a_lo = split_table(np.concatenate([np.cos(ang), np.sin(ang)], 0))
    a_cat = np.concatenate([a_hi, a_lo], 1)
    c_hi, c_lo = split_table(np.concatenate([np.cos(ang.T), np.sin(ang.T)], 1) / LEN)
    c_cat = np.concatenate([c_hi, c_lo, c_hi], 1)
    tw = -2 * np.pi * ((n2[None, :] * (4 * n1[:, None] + 1)) % (4 * LEN)) / (4 * LEN)
    t_re, t_im = np.cos(tw).astype(np.float32), np.sin(tw).astype(np.float32)
    bang = -2 * np.pi * ((n2[:, None] * n2[None, :]) % 256) / 256
    b_hi, b_lo = split_table(np.concatenate([np.cos(bang), np.sin(bang)], 1))
    b_cat = np.concatenate([b_hi, b_lo, b_hi], 0)
    return a_cat, b_cat, c_cat, t_re, t_im


def dot(a, b, dims=(((1,), (0,)), ((), ()))):
    return lax.dot_general(a, b, dims, preferred_element_type=F32)


def split(val):
    hi = val.astype(BF16)
    return hi, (val - hi.astype(F32)).astype(BF16)


def kernel(
    q_hbm, k_hbm, v_hbm, taps_hbm, skip_hbm, w_hbm, g_hbm, a_hbm, b_hbm, c_hbm, tr_hbm, ti_hbm,
    out_ref, gq_ref, gk_ref, gv_ref, gf_ref, gs_ref, gw_ref,
    q_ref, k_ref, v_ref, taps_ref, skip_ref, w_ref, g_ref, a_ref, b_ref, c_ref, tr_ref, ti_ref,
    s0, r0, s1, r1, s2, r2, s3, r3, s4, r4,
    i8, i4, prod, dmix, dgat, gfull, gboth, w_oth, gat_oth,
    sig_re, sig_im, tap_re, tap_im,
    g1, rg, rz, ga, sk, rsk1, sk2, rsk2,
    isem, lsem, ssem, rsem,
):
    me = lax.axis_index("ctx")
    ch = lax.axis_index("ch")
    y, z, x = me // 32, lax.rem(me // 4, NZ), lax.rem(me, NX)
    plane = y * NX + x

    def peer(idx):
        return {"ctx": idx}

    def remote(src, dst, sem, device):
        return pltpu.make_async_remote_copy(
            src_ref=src, dst_ref=dst, send_sem=ssem.at[sem], recv_sem=rsem.at[sem],
            device_id=device, device_id_type=MESH,
        )

    def at_plane(idx):
        return peer(idx // NX * 32 + z * NX + lax.rem(idx, NX))

    def at_z(idx):
        return peer(y * 32 + idx * NX + x)

    plane_order = [lax.rem(plane + step, 16) for step in range(1, 16)]
    z_order = [lax.rem(z + step, NZ) for step in range(1, NZ)]
    sibling = {"ch": 1 - ch}

    bar = pltpu.get_barrier_semaphore()

    def greet(step, carry):
        pl.semaphore_signal(bar, inc=1, device_id=peer(lax.rem(me + 1 + step, NCTX)), device_id_type=MESH)
        return carry

    lax.fori_loop(0, NCTX - 1, greet, 0)
    pl.semaphore_signal(bar, inc=1, device_id=sibling, device_id_type=MESH)

    loads = {}
    pairs = (
        (k_hbm, k_ref), (v_hbm, v_ref), (taps_hbm, taps_ref), (g_hbm, g_ref), (w_hbm, w_ref),
        (q_hbm, q_ref), (a_hbm, a_ref), (tr_hbm, tr_ref), (ti_hbm, ti_ref), (b_hbm, b_ref),
        (c_hbm, c_ref), (skip_hbm, skip_ref),
    )
    for i, (src, dst) in enumerate(pairs):
        loads[i] = pltpu.make_async_copy(src, dst, isem.at[i])
        loads[i].start()

    def interleave(blocks, tmp, dst):
        rows = len(blocks)
        for r, blk in enumerate(blocks):
            tmp[pl.ds(r, 128, stride=rows), :] = blk
        dst[...] = tmp[...].reshape(128, rows, 128).astype(BF16)

    def separate(src, tmp, rows):
        tmp[...] = src[...].astype(F32).reshape(128 * rows, 128)
        return [tmp[pl.ds(r, 128, stride=rows), :] for r in range(rows)]

    def send_all(src, dst, sem, low=0, high=NCTX - 1):
        if low == 0:
            pltpu.make_async_copy(src.at[me], dst.at[me], lsem.at[sem]).start()

        def go(step, carry):
            to = lax.rem(me + 1 + step, NCTX)
            remote(src.at[to], dst.at[me], sem, peer(to)).start()
            return carry

        lax.fori_loop(low, high, go, 0)

    def whole(src, dst, sem):
        return remote(
            src.at[pl.ds(0, NCTX - 1)], dst.at[pl.ds(0, NCTX - 1)], sem, peer(lax.rem(me + 1, NCTX))
        )

    def wait_all(src, dst, sem):
        pltpu.make_async_copy(src.at[me], dst.at[me], lsem.at[sem]).wait()
        whole(src, dst, sem).wait_recv()

    def some(buf, count, sem, device):
        part = buf.at[pl.ds(0, count)]
        return remote(part, part, sem, device)

    def blocks_of(val):
        return [
            val[th * 128:(th + 1) * 128, h * 128:(h + 1) * 128].T for h in range(2) for th in range(2)
        ]

    def tokens_of(blks):
        return jnp.concatenate(
            [jnp.concatenate([blks[th].T, blks[2 + th].T], 1) for th in range(2)], 0
        )

    def forward(blks):
        sig = jnp.concatenate(blks, 1).astype(BF16)
        spec = dot(a_ref[...], jnp.concatenate([sig, sig], 0))
        re, im = spec[:128], spec[128:]
        t_re, t_im = tr_ref[...], ti_ref[...]
        top, bottom = [], []
        for h in range(2):
            u, w = re[:, h * 256:(h + 1) * 256], im[:, h * 256:(h + 1) * 256]
            top.append(u * t_re - w * t_im)
            bottom.append(u * t_im + w * t_re)
        hi, lo = split(jnp.concatenate(top + bottom, 0))
        full = dot(jnp.concatenate([hi, hi, lo], 1), b_ref[...])
        return full[:256, :256] - full[256:, 256:], full[:256, 256:] + full[256:, :256]

    def inverse(re, im):
        hi, lo = split(jnp.concatenate([re, im], 0))
        full = dot(jnp.concatenate([hi, hi, lo], 1), b_ref[...])
        u = full[:256, :256] + full[256:, 256:]
        w = full[256:, :256] - full[:256, 256:]
        t_re, t_im = tr_ref[...], ti_ref[...]
        top, bottom = [], []
        for h in range(2):
            ur, wi = u[h * 128:(h + 1) * 128], w[h * 128:(h + 1) * 128]
            top.append(ur * t_re + wi * t_im)
            bottom.append(wi * t_re - ur * t_im)
        both = jnp.concatenate([jnp.concatenate(top, 1), jnp.concatenate(bottom, 1)], 0)
        hi, lo = split(both)
        sig = dot(c_ref[...], jnp.concatenate([hi, hi, lo], 0))
        return [sig[:, r * 128:(r + 1) * 128] for r in range(4)]

    loads[0].wait()
    loads[1].wait()
    prod[...] = k_ref[...].astype(F32) * v_ref[...].astype(F32)
    interleave(blocks_of(prod[...]), i4, s0)
    loads[2].wait()
    interleave(blocks_of(taps_ref[...]), i4, s1)
    loads[3].wait()
    loads[4].wait()
    pl.semaphore_wait(bar, NCTX)
    g_send = remote(g_ref, gboth, 9, sibling)
    g_send.start()
    w_send = remote(w_ref.at[:, pl.ds(pl.multiple_of((1 - ch) * 256, 256), 256)], w_oth, 10, sibling)
    w_send.start()
    send_all(s0, r0, 0)
    send_all(s1, r1, 1)

    loads[5].wait()
    g_send.wait_recv()
    mine, other = g_ref[...], gboth[...]
    first = ch == 0
    gfull[:, :256] = jnp.where(first, mine.astype(F32), other.astype(F32)).astype(BF16)
    gfull[:, 256:] = jnp.where(first, other.astype(F32), mine.astype(F32)).astype(BF16)
    dgat[...] = dot(gfull[...], w_ref[...], (((1,), (1,)), ((), ())))
    dmix[...] = dgat[...] * q_ref[...].astype(F32)
    interleave(blocks_of(dmix[...]), i4, s2)
    send_all(s2, r2, 2)

    sk[...] = jnp.sum(dmix[...] * prod[...], axis=0, keepdims=True)
    for to in plane_order:
        remote(sk, rsk1.at[plane], 5, at_plane(to)).start()
    for i in range(6, 12):
        loads[i].wait()

    wait_all(s0, r0, 0)
    re, im = forward(separate(r0, i4, 4))
    sig_re[...], sig_im[...] = re, im
    wait_all(s1, r1, 1)
    re, im = forward(separate(r1, i4, 4))
    tap_re[...], tap_im[...] = re, im
    re, im = sig_re[...], sig_im[...]
    conv = inverse(re * tap_re[...] - im * tap_im[...], re * tap_im[...] + im * tap_re[...])
    interleave(conv, i4, s3)
    send_all(s3, r3, 3)

    some(rsk1, 15, 5, at_plane(plane_order[0])).wait_recv()
    rsk1[plane] = sk[...]
    sk2[...] = jnp.sum(rsk1[...], axis=0)
    for to in z_order:
        remote(sk2, rsk2.at[z], 6, at_z(to)).start()

    wait_all(s2, r2, 2)
    re, im = forward(separate(r2, i4, 4))
    lag_p = inverse(re * tap_re[...] + im * tap_im[...], im * tap_re[...] - re * tap_im[...])
    lag_f = inverse(re * sig_re[...] + im * sig_im[...], im * sig_re[...] - re * sig_im[...])
    interleave(lag_p + lag_f, i8, s4)
    if LAG_CUTS[0]:
        send_all(s4, r4, 4, 0, LAG_CUTS[0])

    wait_all(s3, r3, 3)
    skip = skip_ref[...]
    mixed = tokens_of(separate(r3, i4, 4)) + skip * prod[...]
    gated = (q_ref[...].astype(F32) * mixed).astype(BF16)
    full = dot(gated, gfull[...], (((0,), (0,)), ((), ())))
    g1[...] = full.reshape(16, 16, 512).astype(BF16)
    for to in plane_order:
        remote(g1.at[to], rg.at[plane], 7, at_plane(to)).start()
    gat_oth[0] = gated
    gat_send = remote(gat_oth.at[0], gat_oth.at[1], 11, sibling)
    gat_send.start()
    send_all(s4, r4, 4, LAG_CUTS[0], LAG_CUTS[1])
    gq_ref[...] = (dgat[...] * mixed).astype(BF16)
    w_send.wait_recv()
    w_mine = w_ref[:, pl.ds(pl.multiple_of(ch * 256, 256), 256)]
    part = dot(gated, w_mine)
    gat_send.wait_recv()
    out_ref[...] = (part + dot(gat_oth[1], w_oth[...])).astype(BF16)

    some(rg, 15, 7, at_plane(plane_order[0])).wait_recv()
    rg[plane] = g1[plane]
    rz[z] = jnp.sum(rg[...].astype(F32), axis=0).astype(BF16)
    for to in z_order:
        remote(rz.at[z], rz.at[z], 8, at_z(to)).start()
    send_all(s4, r4, 4, LAG_CUTS[1], NCTX - 1)
    some(rsk2, 7, 6, at_z(z_order[0])).wait_recv()
    rsk2[z] = sk2[...]
    gs_ref[...] = jnp.sum(rsk2[...], axis=0) / ROOT
    some(rz, 7, 8, at_z(z_order[0])).wait_recv()
    ga[plane] = (jnp.sum(rz[...].astype(F32), axis=0) / ROOT).astype(BF16)
    for to in plane_order:
        remote(ga.at[plane], ga.at[plane], 12, at_plane(to)).start()

    wait_all(s4, r4, 4)
    blks = separate(r4, i8, 8)
    grad_prod = tokens_of(blks[:4]) + skip * dmix[...]
    gk_ref[...] = (grad_prod * v_ref[...].astype(F32)).astype(BF16)
    gv_ref[...] = (grad_prod * k_ref[...].astype(F32)).astype(BF16)
    gf_ref[...] = tokens_of(blks[4:]) / ROOT

    whole(s0, r0, 0).wait_send()
    whole(s1, r1, 1).wait_send()
    whole(s2, r2, 2).wait_send()
    whole(s3, r3, 3).wait_send()
    whole(s4, r4, 4).wait_send()
    some(rsk1, 15, 5, at_plane(plane_order[0])).wait_send()
    some(rsk2, 7, 6, at_z(z_order[0])).wait_send()
    some(rg, 15, 7, at_plane(plane_order[0])).wait_send()
    some(rz, 7, 8, at_z(z_order[0])).wait_send()
    g_send.wait_send()
    w_send.wait_send()
    gat_send.wait_send()

    last = some(ga, 15, 12, at_plane(plane_order[0]))
    last.wait_recv()
    gw_ref[...] = ga[...].astype(F32).reshape(256, 512)
    last.wait_send()


def finish(*refs):
    count = (len(refs) - 1) // 3
    src, dst, mid, sem = refs[:count], refs[count:2 * count], refs[2 * count:3 * count], refs[-1]
    loads = [pltpu.make_async_copy(src[i], mid[i], sem.at[0, i]) for i in range(count)]
    stores = [pltpu.make_async_copy(mid[i], dst[i], sem.at[1, i]) for i in range(count)]
    for one in loads:
        one.start()
    for load, store in zip(loads, stores):
        load.wait()
        store.start()
    for one in stores:
        one.wait()


def shards(query_act, key_act, value_act, filter_taps, skip_gain, out_weight, out_grad):
    a_cat, b_cat, c_cat, t_re, t_im = (jnp.asarray(t) for t in tables())
    vmem = pl.BlockSpec(memory_space=pltpu.VMEM)
    anywhere = pl.BlockSpec(memory_space=pl.ANY)
    sds = jax.ShapeDtypeStruct
    operands = (
        query_act, key_act, value_act, filter_taps, skip_gain[None, :], out_weight, out_grad,
        a_cat, b_cat, c_cat, t_re, t_im,
    )
    results = (
        sds((256, 256), BF16), sds((256, 256), BF16), sds((256, 256), BF16),
        sds((256, 256), BF16), sds((256, 256), F32), sds((1, 256), F32), sds((256, 512), F32),
    )
    msg4, msg8 = pltpu.VMEM((128, 4, 128), BF16), pltpu.VMEM((128, 8, 128), BF16)
    square, half = pltpu.VMEM((256, 256), F32), pltpu.VMEM((256, 256), BF16)
    outs = pl.pallas_call(
        kernel,
        out_shape=results,
        in_specs=[anywhere] * 12,
        out_specs=[vmem] * 7,
        scratch_shapes=[pltpu.VMEM(op.shape, op.dtype) for op in operands] + [
            msg4, msg4, msg4, msg4, msg4, msg4, msg4, msg4, msg8, msg8,
            pltpu.VMEM((1024, 128), F32), pltpu.VMEM((512, 128), F32),
            square, square, square,
            pltpu.VMEM((256, 512), BF16), half, half, pltpu.VMEM((2, 256, 256), BF16),
            square, square, square, square,
            pltpu.VMEM((16, 16, 512), BF16), pltpu.VMEM((16, 16, 512), BF16),
            pltpu.VMEM((8, 16, 512), BF16), pltpu.VMEM((16, 16, 512), BF16),
            pltpu.VMEM((1, 256), F32), pltpu.VMEM((16, 1, 256), F32),
            pltpu.VMEM((1, 256), F32), pltpu.VMEM((8, 1, 256), F32),
            pltpu.SemaphoreType.DMA((12,)), pltpu.SemaphoreType.DMA((5,)),
            pltpu.SemaphoreType.DMA((13,)), pltpu.SemaphoreType.DMA((13,)),
        ],
        compiler_params=pltpu.CompilerParams(
            collective_id=0, has_side_effects=True, vmem_limit_bytes=56 * 1024 * 1024
        ),
        name="hyena",
    )(*operands)
    outs = pl.pallas_call(
        finish,
        out_shape=results,
        in_specs=[anywhere] * 7,
        out_specs=[anywhere] * 7,
        scratch_shapes=[pltpu.VMEM(res.shape, res.dtype) for res in results]
        + [pltpu.SemaphoreType.DMA((2, 7))],
        name="finish",
    )(*outs)
    out, gq, gk, gv, gf, gs, gw = outs
    return out, gq, gk, gv, gf, gs.reshape(256), gw


def solution(mesh):
    spec = P("ctx", "ch")
    in_specs = (spec, spec, spec, spec, P("ch"), P("ch", None), spec)
    out_specs = (spec, spec, spec, spec, spec, P("ch"), P("ch", None))
    return jax.shard_map(shards, mesh=mesh, in_specs=in_specs, out_specs=out_specs, check_vma=False)
```

```python
import math

import jax
import jax.numpy as jnp
import numpy as np
import ml_dtypes
from jax import lax
from jax.experimental import pallas as pl
from jax.experimental.pallas import tpu as pltpu
from jax.sharding import PartitionSpec as P

MESH = pl.DeviceIdType.MESH
F32, BF16 = jnp.float32, jnp.bfloat16
NCTX = 128
NY, NZ, NX = 4, 8, 4
LEN = 32768
ROOT = math.sqrt(LEN)
LAG_CUTS = (64, 127)
PARTS = 4
WIDTH = 512 // PARTS
SCATTER, ACROSS, GATHER = (7, 13, 16, 17), (8, 14, 18, 19), (12, 15, 20, 21)


def split_table(table):
    table = table.astype(np.float32)
    hi = table.astype(ml_dtypes.bfloat16)
    lo = (table - hi.astype(np.float32)).astype(ml_dtypes.bfloat16)
    return hi, lo


def tables():
    n1 = np.arange(128)
    n2 = np.arange(256)
    ang = -2 * np.pi * ((n1[None, :] * (4 * n1[:, None] + 1)) % 512) / 512
    a_hi, a_lo = split_table(np.concatenate([np.cos(ang), np.sin(ang)], 0))
    a_cat = np.concatenate([a_hi, a_lo], 1)
    c_hi, c_lo = split_table(np.concatenate([np.cos(ang.T), np.sin(ang.T)], 1) / LEN)
    c_cat = np.concatenate([c_hi, c_lo, c_hi], 1)
    tw = -2 * np.pi * ((n2[None, :] * (4 * n1[:, None] + 1)) % (4 * LEN)) / (4 * LEN)
    t_re, t_im = np.cos(tw).astype(np.float32), np.sin(tw).astype(np.float32)
    bang = -2 * np.pi * ((n2[:, None] * n2[None, :]) % 256) / 256
    b_hi, b_lo = split_table(np.concatenate([np.cos(bang), np.sin(bang)], 1))
    b_cat = np.concatenate([b_hi, b_lo, b_hi], 0)
    return a_cat, b_cat, c_cat, t_re, t_im


def dot(a, b, dims=(((1,), (0,)), ((), ()))):
    return lax.dot_general(a, b, dims, preferred_element_type=F32)


def split(val):
    hi = val.astype(BF16)
    return hi, (val - hi.astype(F32)).astype(BF16)


def kernel(
    q_hbm, k_hbm, v_hbm, taps_hbm, skip_hbm, w_hbm, g_hbm, a_hbm, b_hbm, c_hbm, tr_hbm, ti_hbm,
    out_hbm, gq_hbm, gk_hbm, gv_hbm, gf_hbm, gs_hbm, gw_hbm,
    q_ref, k_ref, v_ref, taps_ref, skip_ref, w_ref, g_ref, a_ref, b_ref, c_ref, tr_ref, ti_ref,
    s0, r0, s1, r1, s2, r2, s3, r3, s4, r4,
    i8, i4, prod, dmix, dgat, gfull, gboth, w_oth, gat_oth,
    sig_re, sig_im, tap_re, tap_im,
    g1, rg, rz, ga, sk, rsk1, sk2, rsk2,
    out_ref, gq_ref, gk_ref, gv_ref, gf_ref, gs_ref,
    isem, osem, lsem, ssem, rsem,
):
    me = lax.axis_index("ctx")
    ch = lax.axis_index("ch")
    y, z, x = me // 32, lax.rem(me // 4, NZ), lax.rem(me, NX)
    plane = y * NX + x

    def peer(idx):
        return {"ctx": idx}

    def remote(src, dst, sem, device):
        return pltpu.make_async_remote_copy(
            src_ref=src, dst_ref=dst, send_sem=ssem.at[sem], recv_sem=rsem.at[sem],
            device_id=device, device_id_type=MESH,
        )

    def at_plane(idx):
        return peer(idx // NX * 32 + z * NX + lax.rem(idx, NX))

    def at_z(idx):
        return peer(y * 32 + idx * NX + x)

    plane_order = [lax.rem(plane + step, 16) for step in range(1, 16)]
    z_order = [lax.rem(z + step, NZ) for step in range(1, NZ)]
    sibling = {"ch": 1 - ch}

    bar = pltpu.get_barrier_semaphore()

    def greet(to, carry):
        pl.semaphore_signal(bar, inc=1, device_id=peer(to), device_id_type=MESH)
        return carry

    lax.fori_loop(me + 1, NCTX, greet, 0)
    lax.fori_loop(0, me, greet, 0)
    pl.semaphore_signal(bar, inc=1, device_id=sibling, device_id_type=MESH)

    loads = {}
    pairs = (
        (k_hbm, k_ref), (v_hbm, v_ref), (taps_hbm, taps_ref), (g_hbm, g_ref), (w_hbm, w_ref),
        (q_hbm, q_ref), (a_hbm, a_ref), (tr_hbm, tr_ref), (ti_hbm, ti_ref), (b_hbm, b_ref),
        (c_hbm, c_ref), (skip_hbm, skip_ref),
    )
    for i, (src, dst) in enumerate(pairs):
        loads[i] = pltpu.make_async_copy(src, dst, isem.at[i])
        loads[i].start()

    def interleave(blocks, tmp, dst):
        rows = len(blocks)
        for r, blk in enumerate(blocks):
            tmp[pl.ds(r, 128, stride=rows), :] = blk
        dst[...] = tmp[...].reshape(128, rows, 128).astype(BF16)

    def separate(src, tmp, rows):
        tmp[...] = src[...].astype(F32).reshape(128 * rows, 128)
        return [tmp[pl.ds(r, 128, stride=rows), :] for r in range(rows)]

    def send_all(src, dst, sem, low=0, high=NCTX - 1):
        if low == 0:
            pltpu.make_async_copy(src.at[me], dst.at[me], lsem.at[sem]).start()

        def go(to, carry):
            remote(src.at[to], dst.at[me], sem, peer(to)).start()
            return carry

        if (low, high) == (0, NCTX - 1):
            lax.fori_loop(me + 1, NCTX, go, 0)
            lax.fori_loop(0, me, go, 0)
        else:
            lax.fori_loop(low, high, lambda step, carry: go(lax.rem(me + 1 + step, NCTX), carry), 0)

    def whole(src, dst, sem):
        return remote(
            src.at[pl.ds(0, NCTX - 1)], dst.at[pl.ds(0, NCTX - 1)], sem, peer(lax.rem(me + 1, NCTX))
        )

    def wait_all(src, dst, sem):
        pltpu.make_async_copy(src.at[me], dst.at[me], lsem.at[sem]).wait()
        whole(src, dst, sem).wait_recv()

    def some(buf, count, sem, device):
        part = buf.at[pl.ds(0, count)]
        return remote(part, part, sem, device)

    def some_half(buf, h, count, sem, device):
        part = buf.at[h, pl.ds(0, count)]
        return remote(part, part, sem, device)

    stores = []

    def store(src, dst):
        one = pltpu.make_async_copy(src, dst, osem.at[len(stores)])
        one.start()
        stores.append(one)

    def blocks_of(val):
        return [
            val[th * 128:(th + 1) * 128, h * 128:(h + 1) * 128].T for h in range(2) for th in range(2)
        ]

    def tokens_of(blks):
        return jnp.concatenate(
            [jnp.concatenate([blks[th].T, blks[2 + th].T], 1) for th in range(2)], 0
        )

    def forward(blks):
        sig = jnp.concatenate(blks, 1).astype(BF16)
        spec = dot(a_ref[...], jnp.concatenate([sig, sig], 0))
        re, im = spec[:128], spec[128:]
        t_re, t_im = tr_ref[...], ti_ref[...]
        top, bottom = [], []
        for h in range(2):
            u, w = re[:, h * 256:(h + 1) * 256], im[:, h * 256:(h + 1) * 256]
            top.append(u * t_re - w * t_im)
            bottom.append(u * t_im + w * t_re)
        hi, lo = split(jnp.concatenate(top + bottom, 0))
        full = dot(jnp.concatenate([hi, hi, lo], 1), b_ref[...])
        return full[:256, :256] - full[256:, 256:], full[:256, 256:] + full[256:, :256]

    def inverse(re, im):
        hi, lo = split(jnp.concatenate([re, im], 0))
        full = dot(jnp.concatenate([hi, hi, lo], 1), b_ref[...])
        u = full[:256, :256] + full[256:, 256:]
        w = full[256:, :256] - full[:256, 256:]
        t_re, t_im = tr_ref[...], ti_ref[...]
        top, bottom = [], []
        for h in range(2):
            ur, wi = u[h * 128:(h + 1) * 128], w[h * 128:(h + 1) * 128]
            top.append(ur * t_re + wi * t_im)
            bottom.append(wi * t_re - ur * t_im)
        both = jnp.concatenate([jnp.concatenate(top, 1), jnp.concatenate(bottom, 1)], 0)
        hi, lo = split(both)
        sig = dot(c_ref[...], jnp.concatenate([hi, hi, lo], 0))
        return [sig[:, r * 128:(r + 1) * 128] for r in range(4)]

    loads[0].wait()
    loads[1].wait()
    prod[...] = k_ref[...].astype(F32) * v_ref[...].astype(F32)
    interleave(blocks_of(prod[...]), i4, s0)
    loads[2].wait()
    interleave(blocks_of(taps_ref[...]), i4, s1)
    loads[3].wait()
    loads[4].wait()
    pl.semaphore_wait(bar, NCTX)
    g_send = remote(g_ref, gboth, 9, sibling)
    g_send.start()
    w_send = remote(w_ref.at[:, pl.ds(pl.multiple_of((1 - ch) * 256, 256), 256)], w_oth, 10, sibling)
    w_send.start()
    send_all(s0, r0, 0)
    send_all(s1, r1, 1)

    loads[5].wait()
    g_send.wait_recv()
    mine, other = g_ref[...], gboth[...]
    first = ch == 0
    gfull[:, :256] = jnp.where(first, mine.astype(F32), other.astype(F32)).astype(BF16)
    gfull[:, 256:] = jnp.where(first, other.astype(F32), mine.astype(F32)).astype(BF16)
    dgat[...] = dot(gfull[...], w_ref[...], (((1,), (1,)), ((), ())))
    dmix[...] = dgat[...] * q_ref[...].astype(F32)
    interleave(blocks_of(dmix[...]), i4, s2)
    send_all(s2, r2, 2)

    sk[...] = jnp.sum(dmix[...] * prod[...], axis=0, keepdims=True)
    for to in plane_order:
        remote(sk, rsk1.at[plane], 5, at_plane(to)).start()
    for i in range(6, 12):
        loads[i].wait()

    wait_all(s0, r0, 0)
    re, im = forward(separate(r0, i4, 4))
    sig_re[...], sig_im[...] = re, im
    wait_all(s1, r1, 1)
    re, im = forward(separate(r1, i4, 4))
    tap_re[...], tap_im[...] = re, im
    re, im = sig_re[...], sig_im[...]
    conv = inverse(re * tap_re[...] - im * tap_im[...], re * tap_im[...] + im * tap_re[...])
    interleave(conv, i4, s3)
    send_all(s3, r3, 3)

    some(rsk1, 15, 5, at_plane(plane_order[0])).wait_recv()
    rsk1[plane] = sk[...]
    sk2[...] = jnp.sum(rsk1[...], axis=0)
    for to in z_order:
        remote(sk2, rsk2.at[z], 6, at_z(to)).start()

    wait_all(s2, r2, 2)
    re, im = forward(separate(r2, i4, 4))
    lag_p = inverse(re * tap_re[...] + im * tap_im[...], im * tap_re[...] - re * tap_im[...])
    lag_f = inverse(re * sig_re[...] + im * sig_im[...], im * sig_re[...] - re * sig_im[...])
    interleave(lag_p + lag_f, i8, s4)
    if LAG_CUTS[0]:
        send_all(s4, r4, 4, 0, LAG_CUTS[0])

    wait_all(s3, r3, 3)
    skip = skip_ref[...]
    mixed = tokens_of(separate(r3, i4, 4)) + skip * prod[...]
    gated = (q_ref[...].astype(F32) * mixed).astype(BF16)
    for h in range(PARTS):
        full = dot(gated, gfull[:, h * WIDTH:(h + 1) * WIDTH], (((0,), (0,)), ((), ())))
        g1[h] = full.reshape(16, 16, WIDTH).astype(BF16)
        for to in plane_order:
            remote(g1.at[h, to], rg.at[h, plane], SCATTER[h], at_plane(to)).start()
    gat_oth[0] = gated
    gat_send = remote(gat_oth.at[0], gat_oth.at[1], 11, sibling)
    gat_send.start()
    send_all(s4, r4, 4, LAG_CUTS[0], LAG_CUTS[1])
    gq_ref[...] = (dgat[...] * mixed).astype(BF16)
    store(gq_ref, gq_hbm)
    w_send.wait_recv()
    w_mine = w_ref[:, pl.ds(pl.multiple_of(ch * 256, 256), 256)]
    part = dot(gated, w_mine)
    gat_send.wait_recv()
    out_ref[...] = (part + dot(gat_oth[1], w_oth[...])).astype(BF16)
    store(out_ref, out_hbm)

    for h in range(PARTS):
        some_half(rg, h, 15, SCATTER[h], at_plane(plane_order[0])).wait_recv()
        rg[h, plane] = g1[h, plane]
        rz[h, z] = jnp.sum(rg[h].astype(F32), axis=0).astype(BF16)
        for to in z_order:
            remote(rz.at[h, z], rz.at[h, z], ACROSS[h], at_z(to)).start()
    send_all(s4, r4, 4, LAG_CUTS[1], NCTX - 1)
    some(rsk2, 7, 6, at_z(z_order[0])).wait_recv()
    rsk2[z] = sk2[...]
    gs_ref[...] = jnp.sum(rsk2[...], axis=0) / ROOT
    store(gs_ref, gs_hbm)
    for h in range(PARTS):
        some_half(rz, h, 7, ACROSS[h], at_z(z_order[0])).wait_recv()
        ga[h, plane] = (jnp.sum(rz[h].astype(F32), axis=0) / ROOT).astype(BF16)
        for to in plane_order:
            remote(ga.at[h, plane], ga.at[h, plane], GATHER[h], at_plane(to)).start()

    wait_all(s4, r4, 4)
    blks = separate(r4, i8, 8)
    grad_prod = tokens_of(blks[:4]) + skip * dmix[...]
    gk_ref[...] = (grad_prod * v_ref[...].astype(F32)).astype(BF16)
    gv_ref[...] = (grad_prod * k_ref[...].astype(F32)).astype(BF16)
    gf_ref[...] = tokens_of(blks[4:]).astype(BF16)
    store(gk_ref, gk_hbm)
    store(gv_ref, gv_hbm)
    store(gf_ref, gf_hbm)

    whole(s0, r0, 0).wait_send()
    whole(s1, r1, 1).wait_send()
    whole(s2, r2, 2).wait_send()
    whole(s3, r3, 3).wait_send()
    whole(s4, r4, 4).wait_send()
    some(rsk1, 15, 5, at_plane(plane_order[0])).wait_send()
    some(rsk2, 7, 6, at_z(z_order[0])).wait_send()
    for h in range(PARTS):
        some_half(rg, h, 15, SCATTER[h], at_plane(plane_order[0])).wait_send()
        some_half(rz, h, 7, ACROSS[h], at_z(z_order[0])).wait_send()
    g_send.wait_send()
    w_send.wait_send()
    gat_send.wait_send()

    for h in range(PARTS):
        last = some_half(ga, h, 15, GATHER[h], at_plane(plane_order[0]))
        last.wait_recv()
        store(ga.at[h], gw_hbm.at[h])
        last.wait_send()
    for one in stores:
        one.wait()


def finish(*refs):
    src, dst, mid, taps, wide, sem = refs[:7], refs[7:14], refs[14:21], refs[21], refs[22], refs[23]
    last = list(mid[:4]) + [taps, mid[5], wide]
    loads = [pltpu.make_async_copy(src[i], mid[i], sem.at[0, i]) for i in range(7)]
    stores = [pltpu.make_async_copy(last[i], dst[i], sem.at[1, i]) for i in range(7)]
    order = (0, 6, 4, 1, 2, 3, 5)
    for i in order:
        loads[i].start()
    for i in order:
        loads[i].wait()
        if i == 6:
            for h in range(PARTS):
                wide[:, h * WIDTH:(h + 1) * WIDTH] = mid[6][h].astype(F32).reshape(256, WIDTH)
        if i == 4:
            taps[...] = mid[4][...].astype(F32) / ROOT
        stores[i].start()
    for one in stores:
        one.wait()


def shards(query_act, key_act, value_act, filter_taps, skip_gain, out_weight, out_grad):
    a_cat, b_cat, c_cat, t_re, t_im = (jnp.asarray(t) for t in tables())
    anywhere = pl.BlockSpec(memory_space=pl.ANY)
    sds = jax.ShapeDtypeStruct
    operands = (
        query_act, key_act, value_act, filter_taps, skip_gain[None, :], out_weight, out_grad,
        a_cat, b_cat, c_cat, t_re, t_im,
    )
    results = (
        sds((256, 256), BF16), sds((256, 256), BF16), sds((256, 256), BF16),
        sds((256, 256), BF16), sds((256, 256), F32), sds((1, 256), F32), sds((256, 512), F32),
    )
    msg4, msg8 = pltpu.VMEM((128, 4, 128), BF16), pltpu.VMEM((128, 8, 128), BF16)
    square, half = pltpu.VMEM((256, 256), F32), pltpu.VMEM((256, 256), BF16)
    halves = sds((PARTS, 16, 16, WIDTH), BF16)
    middle = results[:4] + (sds((256, 256), BF16), results[5], halves)
    outs = pl.pallas_call(
        kernel,
        out_shape=middle,
        in_specs=[anywhere] * 12,
        out_specs=[anywhere] * 7,
        scratch_shapes=[pltpu.VMEM(op.shape, op.dtype) for op in operands] + [
            msg4, msg4, msg4, msg4, msg4, msg4, msg4, msg4, msg8, msg8,
            pltpu.VMEM((1024, 128), F32), pltpu.VMEM((512, 128), F32),
            square, square, square,
            pltpu.VMEM((256, 512), BF16), half, half, pltpu.VMEM((2, 256, 256), BF16),
            square, square, square, square,
            pltpu.VMEM((PARTS, 16, 16, WIDTH), BF16), pltpu.VMEM((PARTS, 16, 16, WIDTH), BF16),
            pltpu.VMEM((PARTS, 8, 16, WIDTH), BF16), pltpu.VMEM((PARTS, 16, 16, WIDTH), BF16),
            pltpu.VMEM((1, 256), F32), pltpu.VMEM((16, 1, 256), F32),
            pltpu.VMEM((1, 256), F32), pltpu.VMEM((8, 1, 256), F32),
            half, half, half, half, half, pltpu.VMEM((1, 256), F32),
            pltpu.SemaphoreType.DMA((12,)), pltpu.SemaphoreType.DMA((12,)), pltpu.SemaphoreType.DMA((5,)),
            pltpu.SemaphoreType.DMA((22,)), pltpu.SemaphoreType.DMA((22,)),
        ],
        compiler_params=pltpu.CompilerParams(
            collective_id=0, has_side_effects=True, vmem_limit_bytes=56 * 1024 * 1024
        ),
        name="hyena",
    )(*operands)
    outs = pl.pallas_call(
        finish,
        out_shape=results,
        in_specs=[anywhere] * 7,
        out_specs=[anywhere] * 7,
        scratch_shapes=[pltpu.VMEM(res.shape, res.dtype) for res in middle]
        + [pltpu.VMEM((256, 256), F32), pltpu.VMEM((256, 512), F32), pltpu.SemaphoreType.DMA((2, 7))],
        name="finish",
    )(*outs)
    out, gq, gk, gv, gf, gs, gw = outs
    return out, gq, gk, gv, gf, gs.reshape(256), gw


def solution(mesh):
    spec = P("ctx", "ch")
    in_specs = (spec, spec, spec, spec, P("ch"), P("ch", None), spec)
    out_specs = (spec, spec, spec, spec, spec, P("ch"), P("ch", None))
    return jax.shard_map(shards, mesh=mesh, in_specs=in_specs, out_specs=out_specs, check_vma=False)
```

```python
import math

import jax
import jax.numpy as jnp
import numpy as np
import ml_dtypes
from jax import lax
from jax.experimental import pallas as pl
from jax.experimental.pallas import tpu as pltpu
from jax.sharding import PartitionSpec as P

MESH = pl.DeviceIdType.MESH
F32, BF16 = jnp.float32, jnp.bfloat16
NCTX = 128
NY, NZ, NX = 4, 8, 4
LEN = 32768
ROOT = math.sqrt(LEN)
LAG_CUTS = (64, 127)
PARTS = 4
WIDTH = 512 // PARTS
SCATTER, ACROSS, GATHER = (7, 13, 16, 17), (8, 14, 18, 19), (12, 15, 20, 21)


def split_table(table):
    table = table.astype(np.float32)
    hi = table.astype(ml_dtypes.bfloat16)
    lo = (table - hi.astype(np.float32)).astype(ml_dtypes.bfloat16)
    return hi, lo


def tables():
    n1 = np.arange(128)
    n2 = np.arange(256)
    ang = -2 * np.pi * ((n1[None, :] * (4 * n1[:, None] + 1)) % 512) / 512
    a_hi, a_lo = split_table(np.concatenate([np.cos(ang), np.sin(ang)], 0))
    a_cat = np.concatenate([a_hi, a_lo], 1)
    c_hi, c_lo = split_table(np.concatenate([np.cos(ang.T), np.sin(ang.T)], 1) / LEN)
    c_cat = np.concatenate([c_hi, c_lo, c_hi], 1)
    tw = -2 * np.pi * ((n2[None, :] * (4 * n1[:, None] + 1)) % (4 * LEN)) / (4 * LEN)
    t_re, t_im = np.cos(tw).astype(np.float32), np.sin(tw).astype(np.float32)
    bang = -2 * np.pi * ((n2[:, None] * n2[None, :]) % 256) / 256
    b_re, b_im = np.cos(bang), np.sin(bang)
    b_hi, b_lo = split_table(np.block([[b_re, b_im], [-b_im, b_re]]))
    b_cat = np.concatenate([b_hi, b_lo, b_hi], 0)
    return a_cat, b_cat, c_cat, t_re, t_im


def dot(a, b, dims=(((1,), (0,)), ((), ()))):
    return lax.dot_general(a, b, dims, preferred_element_type=F32)


def split(val):
    hi = val.astype(BF16)
    return hi, (val - hi.astype(F32)).astype(BF16)


def kernel(
    q_hbm, k_hbm, v_hbm, taps_hbm, skip_hbm, w_hbm, g_hbm, a_hbm, b_hbm, c_hbm, tr_hbm, ti_hbm,
    out_hbm, gq_hbm, gk_hbm, gv_hbm, gf_hbm, gs_hbm, gw_hbm,
    q_ref, k_ref, v_ref, taps_ref, skip_ref, w_ref, g_ref, a_ref, b_ref, c_ref, tr_ref, ti_ref,
    s0, r0, s1, r1, s2, r2, s3, r3, s4, r4,
    i8, i4, prod, dmix, dgat, base_t, q_t, gfull, gboth, w_oth, gat_oth,
    sig_re, sig_im, tap_re, tap_im,
    g1, rg, rz, ga, sk, rsk1, sk2, rsk2,
    out_ref, gq_ref, gk_ref, gv_ref, gf_ref, gs_ref,
    isem, osem, lsem, ssem, rsem,
):
    me = lax.axis_index("ctx")
    ch = lax.axis_index("ch")
    y, z, x = me // 32, lax.rem(me // 4, NZ), lax.rem(me, NX)
    plane = y * NX + x

    def peer(idx):
        return {"ctx": idx}

    def remote(src, dst, sem, device):
        return pltpu.make_async_remote_copy(
            src_ref=src, dst_ref=dst, send_sem=ssem.at[sem], recv_sem=rsem.at[sem],
            device_id=device, device_id_type=MESH,
        )

    def at_plane(idx):
        return peer(idx // NX * 32 + z * NX + lax.rem(idx, NX))

    def at_z(idx):
        return peer(y * 32 + idx * NX + x)

    plane_order = [lax.rem(plane + step, 16) for step in range(1, 16)]
    z_order = [lax.rem(z + step, NZ) for step in range(1, NZ)]
    sibling = {"ch": 1 - ch}

    bar = pltpu.get_barrier_semaphore()

    def greet(to, carry):
        pl.semaphore_signal(bar, inc=1, device_id=peer(to), device_id_type=MESH)
        return carry

    lax.fori_loop(me + 1, NCTX, greet, 0)
    lax.fori_loop(0, me, greet, 0)
    pl.semaphore_signal(bar, inc=1, device_id=sibling, device_id_type=MESH)

    loads = {}
    pairs = (
        (k_hbm, k_ref), (v_hbm, v_ref), (taps_hbm, taps_ref), (g_hbm, g_ref), (w_hbm, w_ref),
        (q_hbm, q_ref), (a_hbm, a_ref), (tr_hbm, tr_ref), (ti_hbm, ti_ref), (b_hbm, b_ref),
        (c_hbm, c_ref), (skip_hbm, skip_ref),
    )
    for i, (src, dst) in enumerate(pairs):
        loads[i] = pltpu.make_async_copy(src, dst, isem.at[i])
        loads[i].start()

    def interleave(blocks, tmp, dst):
        rows = len(blocks)
        for r, blk in enumerate(blocks):
            tmp[pl.ds(r, 128, stride=rows), :] = blk
        dst[...] = tmp[...].reshape(128, rows, 128).astype(BF16)

    def separate(src, tmp, rows):
        tmp[...] = src[...].astype(F32).reshape(128 * rows, 128)
        return [tmp[pl.ds(r, 128, stride=rows), :] for r in range(rows)]

    def send_all(src, dst, sem, low=0, high=NCTX - 1):
        if low == 0:
            pltpu.make_async_copy(src.at[me], dst.at[me], lsem.at[sem]).start()

        def go(to, carry):
            remote(src.at[to], dst.at[me], sem, peer(to)).start()
            return carry

        if (low, high) == (0, NCTX - 1):
            lax.fori_loop(me + 1, NCTX, go, 0)
            lax.fori_loop(0, me, go, 0)
        else:
            lax.fori_loop(low, high, lambda step, carry: go(lax.rem(me + 1 + step, NCTX), carry), 0)

    def whole(src, dst, sem):
        return remote(
            src.at[pl.ds(0, NCTX - 1)], dst.at[pl.ds(0, NCTX - 1)], sem, peer(lax.rem(me + 1, NCTX))
        )

    def wait_all(src, dst, sem):
        pltpu.make_async_copy(src.at[me], dst.at[me], lsem.at[sem]).wait()
        whole(src, dst, sem).wait_recv()

    def some(buf, count, sem, device):
        part = buf.at[pl.ds(0, count)]
        return remote(part, part, sem, device)

    def some_half(buf, h, count, sem, device):
        part = buf.at[h, pl.ds(0, count)]
        return remote(part, part, sem, device)

    stores = []

    def store(src, dst):
        one = pltpu.make_async_copy(src, dst, osem.at[len(stores)])
        one.start()
        stores.append(one)

    def blocks_of(val):
        return [
            val[th * 128:(th + 1) * 128, h * 128:(h + 1) * 128].T for h in range(2) for th in range(2)
        ]

    def channels_of(blks):
        return jnp.concatenate(
            [jnp.concatenate([blks[2 * h], blks[2 * h + 1]], 1) for h in range(2)], 0
        )

    def tokens_of(blks):
        return jnp.concatenate(
            [jnp.concatenate([blks[th].T, blks[2 + th].T], 1) for th in range(2)], 0
        )

    def rotate(left, right):
        (lh, ll), (rh, rl) = split(left), split(right)
        return dot(jnp.concatenate([lh, rh, lh, rh, ll, rl], 1), b_ref[...])

    def forward(blks):
        sig = jnp.concatenate(blks, 1).astype(BF16)
        spec = dot(a_ref[...], jnp.concatenate([sig, sig], 0))
        re, im = spec[:128], spec[128:]
        t_re, t_im = tr_ref[...], ti_ref[...]
        top, bottom = [], []
        for h in range(2):
            u, w = re[:, h * 256:(h + 1) * 256], im[:, h * 256:(h + 1) * 256]
            top.append(u * t_re - w * t_im)
            bottom.append(u * t_im + w * t_re)
        full = rotate(jnp.concatenate(top, 0), jnp.concatenate(bottom, 0))
        return full[:, :256], full[:, 256:]

    def inverse(re, im):
        full = rotate(im, re)
        u, w = full[:, 256:], full[:, :256]
        t_re, t_im = tr_ref[...], ti_ref[...]
        top, bottom = [], []
        for h in range(2):
            ur, wi = u[h * 128:(h + 1) * 128], w[h * 128:(h + 1) * 128]
            top.append(ur * t_re + wi * t_im)
            bottom.append(wi * t_re - ur * t_im)
        both = jnp.concatenate([jnp.concatenate(top, 1), jnp.concatenate(bottom, 1)], 0)
        hi, lo = split(both)
        sig = dot(c_ref[...], jnp.concatenate([hi, hi, lo], 0))
        return [sig[:, r * 128:(r + 1) * 128] for r in range(4)]

    loads[0].wait()
    loads[1].wait()
    prod[...] = k_ref[...].astype(F32) * v_ref[...].astype(F32)
    interleave(blocks_of(prod[...]), i4, s0)
    loads[2].wait()
    interleave(blocks_of(taps_ref[...]), i4, s1)
    loads[3].wait()
    loads[4].wait()
    pl.semaphore_wait(bar, NCTX)
    g_send = remote(g_ref, gboth, 9, sibling)
    g_send.start()
    w_send = remote(w_ref.at[:, pl.ds(pl.multiple_of((1 - ch) * 256, 256), 256)], w_oth, 10, sibling)
    w_send.start()
    send_all(s0, r0, 0)
    send_all(s1, r1, 1)

    loads[5].wait()
    g_send.wait_recv()
    mine, other = g_ref[...], gboth[...]
    first = ch == 0
    gfull[:, :256] = jnp.where(first, mine.astype(F32), other.astype(F32)).astype(BF16)
    gfull[:, 256:] = jnp.where(first, other.astype(F32), mine.astype(F32)).astype(BF16)
    dgat[...] = dot(gfull[...], w_ref[...], (((1,), (1,)), ((), ())))
    dmix[...] = dgat[...] * q_ref[...].astype(F32)
    interleave(blocks_of(dmix[...]), i4, s2)
    loads[11].wait()
    base_t[...] = channels_of(blocks_of(skip_ref[...] * prod[...]))
    q_t[...] = channels_of(blocks_of(q_ref[...].astype(F32)))
    send_all(s2, r2, 2)

    sk[...] = jnp.sum(dmix[...] * prod[...], axis=0, keepdims=True)
    for to in plane_order:
        remote(sk, rsk1.at[plane], 5, at_plane(to)).start()
    for i in range(6, 11):
        loads[i].wait()

    wait_all(s0, r0, 0)
    re, im = forward(separate(r0, i4, 4))
    sig_re[...], sig_im[...] = re, im
    wait_all(s1, r1, 1)
    re, im = forward(separate(r1, i4, 4))
    tap_re[...], tap_im[...] = re, im
    re, im = sig_re[...], sig_im[...]
    conv = inverse(re * tap_re[...] - im * tap_im[...], re * tap_im[...] + im * tap_re[...])
    interleave(conv, i4, s3)
    send_all(s3, r3, 3)

    some(rsk1, 15, 5, at_plane(plane_order[0])).wait_recv()
    rsk1[plane] = sk[...]
    sk2[...] = jnp.sum(rsk1[...], axis=0)
    for to in z_order:
        remote(sk2, rsk2.at[z], 6, at_z(to)).start()

    wait_all(s2, r2, 2)
    re, im = forward(separate(r2, i4, 4))
    lag_p = inverse(re * tap_re[...] + im * tap_im[...], im * tap_re[...] - re * tap_im[...])
    lag_f = inverse(re * sig_re[...] + im * sig_im[...], im * sig_re[...] - re * sig_im[...])
    interleave(lag_p + lag_f, i8, s4)
    if LAG_CUTS[0]:
        send_all(s4, r4, 4, 0, LAG_CUTS[0])

    wait_all(s3, r3, 3)
    mixed_t = channels_of(separate(r3, i4, 4)) + base_t[...]
    gated_t = (q_t[...] * mixed_t).astype(BF16)
    for h in range(PARTS):
        full = dot(gated_t, gfull[:, h * WIDTH:(h + 1) * WIDTH])
        g1[h] = full.reshape(16, 16, WIDTH).astype(BF16)
        for to in plane_order:
            remote(g1.at[h, to], rg.at[h, plane], SCATTER[h], at_plane(to)).start()
    gat_oth[0] = gated_t
    gat_send = remote(gat_oth.at[0], gat_oth.at[1], 11, sibling)
    gat_send.start()
    send_all(s4, r4, 4, LAG_CUTS[0], LAG_CUTS[1])
    mixed = tokens_of(
        [mixed_t[h * 128:(h + 1) * 128, th * 128:(th + 1) * 128] for h in range(2) for th in range(2)]
    )
    gq_ref[...] = (dgat[...] * mixed).astype(BF16)
    store(gq_ref, gq_hbm)
    w_send.wait_recv()
    w_mine = w_ref[:, pl.ds(pl.multiple_of(ch * 256, 256), 256)]
    turned = (((0,), (0,)), ((), ()))
    part = dot(gated_t, w_mine, turned)
    gat_send.wait_recv()
    out_ref[...] = (part + dot(gat_oth[1], w_oth[...], turned)).astype(BF16)
    store(out_ref, out_hbm)

    for h in range(PARTS):
        some_half(rg, h, 15, SCATTER[h], at_plane(plane_order[0])).wait_recv()
        rg[h, plane] = g1[h, plane]
        rz[h, z] = jnp.sum(rg[h].astype(F32), axis=0).astype(BF16)
        for to in z_order:
            remote(rz.at[h, z], rz.at[h, z], ACROSS[h], at_z(to)).start()
    send_all(s4, r4, 4, LAG_CUTS[1], NCTX - 1)
    some(rsk2, 7, 6, at_z(z_order[0])).wait_recv()
    rsk2[z] = sk2[...]
    gs_ref[...] = jnp.sum(rsk2[...], axis=0) / ROOT
    store(gs_ref, gs_hbm)
    for h in range(PARTS):
        some_half(rz, h, 7, ACROSS[h], at_z(z_order[0])).wait_recv()
        ga[h, plane] = (jnp.sum(rz[h].astype(F32), axis=0) / ROOT).astype(BF16)
        for to in plane_order:
            remote(ga.at[h, plane], ga.at[h, plane], GATHER[h], at_plane(to)).start()

    wait_all(s4, r4, 4)
    blks = separate(r4, i8, 8)
    grad_prod = tokens_of(blks[:4]) + skip_ref[...] * dmix[...]
    gk_ref[...] = (grad_prod * v_ref[...].astype(F32)).astype(BF16)
    gv_ref[...] = (grad_prod * k_ref[...].astype(F32)).astype(BF16)
    gf_ref[...] = tokens_of(blks[4:]).astype(BF16)
    store(gk_ref, gk_hbm)
    store(gv_ref, gv_hbm)
    store(gf_ref, gf_hbm)

    whole(s0, r0, 0).wait_send()
    whole(s1, r1, 1).wait_send()
    whole(s2, r2, 2).wait_send()
    whole(s3, r3, 3).wait_send()
    whole(s4, r4, 4).wait_send()
    some(rsk1, 15, 5, at_plane(plane_order[0])).wait_send()
    some(rsk2, 7, 6, at_z(z_order[0])).wait_send()
    for h in range(PARTS):
        some_half(rg, h, 15, SCATTER[h], at_plane(plane_order[0])).wait_send()
        some_half(rz, h, 7, ACROSS[h], at_z(z_order[0])).wait_send()
    g_send.wait_send()
    w_send.wait_send()
    gat_send.wait_send()

    for h in range(PARTS):
        last = some_half(ga, h, 15, GATHER[h], at_plane(plane_order[0]))
        last.wait_recv()
        store(ga.at[h], gw_hbm.at[h])
        last.wait_send()
    for one in stores:
        one.wait()


def finish(*refs):
    src, dst, mid, taps, wide, sem = refs[:7], refs[7:14], refs[14:21], refs[21], refs[22], refs[23]
    last = list(mid[:4]) + [taps, mid[5]]
    columns = [slice(h * WIDTH, (h + 1) * WIDTH) for h in range(PARTS)]
    loads = [pltpu.make_async_copy(src[i], mid[i], sem.at[0, i]) for i in range(6)]
    parts = [
        pltpu.make_async_copy(src[6].at[h], mid[6].at[h], sem.at[0, 6 + h]) for h in range(PARTS)
    ]
    stores = [pltpu.make_async_copy(last[i], dst[i], sem.at[1, i]) for i in range(6)]
    outs = [
        pltpu.make_async_copy(wide.at[:, columns[h]], dst[6].at[:, columns[h]], sem.at[1, 6 + h])
        for h in range(PARTS)
    ]
    for one in parts[:2] + [loads[4]] + parts[2:] + loads[:4] + [loads[5]]:
        one.start()
    for h in range(PARTS):
        parts[h].wait()
        wide[:, columns[h]] = mid[6][h].astype(F32).reshape(256, WIDTH)
        outs[h].start()
        if h == 1:
            loads[4].wait()
            taps[...] = mid[4][...].astype(F32) / ROOT
            stores[4].start()
    for i in (0, 1, 2, 3, 5):
        loads[i].wait()
        stores[i].start()
    for one in stores + outs:
        one.wait()


def shards(query_act, key_act, value_act, filter_taps, skip_gain, out_weight, out_grad):
    a_cat, b_cat, c_cat, t_re, t_im = (jnp.asarray(t) for t in tables())
    anywhere = pl.BlockSpec(memory_space=pl.ANY)
    sds = jax.ShapeDtypeStruct
    operands = (
        query_act, key_act, value_act, filter_taps, skip_gain[None, :], out_weight, out_grad,
        a_cat, b_cat, c_cat, t_re, t_im,
    )
    results = (
        sds((256, 256), BF16), sds((256, 256), BF16), sds((256, 256), BF16),
        sds((256, 256), BF16), sds((256, 256), F32), sds((1, 256), F32), sds((256, 512), F32),
    )
    msg4, msg8 = pltpu.VMEM((128, 4, 128), BF16), pltpu.VMEM((128, 8, 128), BF16)
    square, half = pltpu.VMEM((256, 256), F32), pltpu.VMEM((256, 256), BF16)
    halves = sds((PARTS, 16, 16, WIDTH), BF16)
    middle = results[:4] + (sds((256, 256), BF16), results[5], halves)
    outs = pl.pallas_call(
        kernel,
        out_shape=middle,
        in_specs=[anywhere] * 12,
        out_specs=[anywhere] * 7,
        scratch_shapes=[pltpu.VMEM(op.shape, op.dtype) for op in operands] + [
            msg4, msg4, msg4, msg4, msg4, msg4, msg4, msg4, msg8, msg8,
            pltpu.VMEM((1024, 128), F32), pltpu.VMEM((512, 128), F32),
            square, square, square, square, square,
            pltpu.VMEM((256, 512), BF16), half, half, pltpu.VMEM((2, 256, 256), BF16),
            square, square, square, square,
            pltpu.VMEM((PARTS, 16, 16, WIDTH), BF16), pltpu.VMEM((PARTS, 16, 16, WIDTH), BF16),
            pltpu.VMEM((PARTS, 8, 16, WIDTH), BF16), pltpu.VMEM((PARTS, 16, 16, WIDTH), BF16),
            pltpu.VMEM((1, 256), F32), pltpu.VMEM((16, 1, 256), F32),
            pltpu.VMEM((1, 256), F32), pltpu.VMEM((8, 1, 256), F32),
            half, half, half, half, half, pltpu.VMEM((1, 256), F32),
            pltpu.SemaphoreType.DMA((12,)), pltpu.SemaphoreType.DMA((12,)), pltpu.SemaphoreType.DMA((5,)),
            pltpu.SemaphoreType.DMA((22,)), pltpu.SemaphoreType.DMA((22,)),
        ],
        compiler_params=pltpu.CompilerParams(
            collective_id=0, has_side_effects=True, vmem_limit_bytes=56 * 1024 * 1024
        ),
        name="hyena",
    )(*operands)
    outs = pl.pallas_call(
        finish,
        out_shape=results,
        in_specs=[anywhere] * 7,
        out_specs=[anywhere] * 7,
        scratch_shapes=[pltpu.VMEM(res.shape, res.dtype) for res in middle]
        + [pltpu.VMEM((256, 256), F32), pltpu.VMEM((256, 512), F32), pltpu.SemaphoreType.DMA((2, 6 + PARTS))],
        name="finish",
    )(*outs)
    out, gq, gk, gv, gf, gs, gw = outs
    return out, gq, gk, gv, gf, gs.reshape(256), gw


def solution(mesh):
    spec = P("ctx", "ch")
    in_specs = (spec, spec, spec, spec, P("ch"), P("ch", None), spec)
    out_specs = (spec, spec, spec, spec, spec, P("ch"), P("ch", None))
    return jax.shard_map(shards, mesh=mesh, in_specs=in_specs, out_specs=out_specs, check_vma=False)
```

```python
import math

import jax
import jax.numpy as jnp
import numpy as np
import ml_dtypes
from jax import lax
from jax.experimental import pallas as pl
from jax.experimental.pallas import tpu as pltpu
from jax.sharding import PartitionSpec as P

MESH = pl.DeviceIdType.MESH
F32, BF16 = jnp.float32, jnp.bfloat16
NCTX = 128
NY, NZ, NX = 4, 8, 4
LEN = 32768
ROOT = math.sqrt(LEN)
LAG_CUTS = (64, 127)
PARTS = 4
WIDTH = 512 // PARTS
SCATTER, ACROSS, GATHER = (7, 13, 16, 17), (8, 14, 18, 19), (12, 15, 20, 21)


def split_table(table):
    table = table.astype(np.float32)
    hi = table.astype(ml_dtypes.bfloat16)
    lo = (table - hi.astype(np.float32)).astype(ml_dtypes.bfloat16)
    return hi, lo


def tables():
    n1 = np.arange(128)
    n2 = np.arange(256)
    ang = -2 * np.pi * ((n1[None, :] * (4 * n1[:, None] + 1)) % 512) / 512
    a_hi, a_lo = split_table(np.concatenate([np.cos(ang), np.sin(ang)], 0))
    a_cat = np.concatenate([a_hi, a_lo], 1)
    c_hi, c_lo = split_table(np.concatenate([np.cos(ang.T), np.sin(ang.T)], 1) / LEN)
    c_cat = np.concatenate([c_hi, c_lo, c_hi], 1)
    tw = -2 * np.pi * ((n2[None, :] * (4 * n1[:, None] + 1)) % (4 * LEN)) / (4 * LEN)
    t_re, t_im = np.cos(tw).astype(np.float32), np.sin(tw).astype(np.float32)
    bang = -2 * np.pi * ((n2[:, None] * n2[None, :]) % 256) / 256
    b_re, b_im = np.cos(bang), np.sin(bang)
    b_hi, b_lo = split_table(np.block([[b_re, b_im], [-b_im, b_re]]))
    b_cat = np.concatenate([b_hi, b_lo, b_hi], 0)
    return a_cat, b_cat, c_cat, t_re, t_im


def dot(a, b, dims=(((1,), (0,)), ((), ()))):
    return lax.dot_general(a, b, dims, preferred_element_type=F32)


def split(val):
    hi = val.astype(BF16)
    return hi, (val - hi.astype(F32)).astype(BF16)


def kernel(
    q_hbm, k_hbm, v_hbm, taps_hbm, skip_hbm, w_hbm, g_hbm, a_hbm, b_hbm, c_hbm, tr_hbm, ti_hbm,
    out_hbm, gq_hbm, gk_hbm, gv_hbm, gf_hbm, gs_hbm, gw_hbm,
    q_ref, k_ref, v_ref, taps_ref, skip_ref, w_ref, g_ref, a_ref, b_ref, c_ref, tr_ref, ti_ref,
    s0, r0, s1, r1, s2, r2, s3, r3, s4, r4,
    i8, i4, prod, dmix, dgat, base_t, q_t, gfull, gboth, w_oth, gat_oth,
    sig_re, sig_im, tap_re, tap_im,
    g1, rg, rz, ga, sk, rsk1, sk2, rsk2,
    out_ref, gq_ref, gk_ref, gv_ref, gf_ref, gs_ref,
    isem, osem, lsem, ssem, rsem,
):
    me = lax.axis_index("ctx")
    ch = lax.axis_index("ch")
    y, z, x = me // 32, lax.rem(me // 4, NZ), lax.rem(me, NX)
    plane = y * NX + x

    def peer(idx):
        return {"ctx": idx}

    def remote(src, dst, sem, device):
        return pltpu.make_async_remote_copy(
            src_ref=src, dst_ref=dst, send_sem=ssem.at[sem], recv_sem=rsem.at[sem],
            device_id=device, device_id_type=MESH,
        )

    def at_plane(idx):
        return peer(idx // NX * 32 + z * NX + lax.rem(idx, NX))

    def at_z(idx):
        return peer(y * 32 + idx * NX + x)

    plane_order = [lax.rem(plane + step, 16) for step in range(1, 16)]
    z_order = [lax.rem(z + step, NZ) for step in range(1, NZ)]
    sibling = {"ch": 1 - ch}

    bar = pltpu.get_barrier_semaphore()

    def greet(to, carry):
        pl.semaphore_signal(bar, inc=1, device_id=peer(to), device_id_type=MESH)
        return carry

    lax.fori_loop(me + 1, NCTX, greet, 0)
    lax.fori_loop(0, me, greet, 0)
    pl.semaphore_signal(bar, inc=1, device_id=sibling, device_id_type=MESH)

    loads = {}
    pairs = (
        (k_hbm, k_ref), (v_hbm, v_ref), (taps_hbm, taps_ref), (g_hbm, g_ref), (w_hbm, w_ref),
        (q_hbm, q_ref), (a_hbm, a_ref), (tr_hbm, tr_ref), (ti_hbm, ti_ref), (b_hbm, b_ref),
        (c_hbm, c_ref), (skip_hbm, skip_ref),
    )
    for i, (src, dst) in enumerate(pairs):
        loads[i] = pltpu.make_async_copy(src, dst, isem.at[i])
        loads[i].start()

    def interleave(blocks, tmp, dst):
        rows = len(blocks)
        for r, blk in enumerate(blocks):
            tmp[pl.ds(r, 128, stride=rows), :] = blk
        dst[...] = tmp[...].reshape(128, rows, 128).astype(BF16)

    def separate(src, tmp, rows):
        tmp[...] = src[...].astype(F32).reshape(128 * rows, 128)
        return [tmp[pl.ds(r, 128, stride=rows), :] for r in range(rows)]

    def send_all(src, dst, sem, low=0, high=NCTX - 1):
        if low == 0:
            pltpu.make_async_copy(src.at[me], dst.at[me], lsem.at[sem]).start()

        def go(to, carry):
            remote(src.at[to], dst.at[me], sem, peer(to)).start()
            return carry

        if (low, high) == (0, NCTX - 1):
            lax.fori_loop(me + 1, NCTX, go, 0)
            lax.fori_loop(0, me, go, 0)
        else:
            lax.fori_loop(low, high, lambda step, carry: go(lax.rem(me + 1 + step, NCTX), carry), 0)

    def whole(src, dst, sem):
        return remote(
            src.at[pl.ds(0, NCTX - 1)], dst.at[pl.ds(0, NCTX - 1)], sem, peer(lax.rem(me + 1, NCTX))
        )

    def wait_all(src, dst, sem):
        pltpu.make_async_copy(src.at[me], dst.at[me], lsem.at[sem]).wait()
        whole(src, dst, sem).wait_recv()

    def some(buf, count, sem, device):
        part = buf.at[pl.ds(0, count)]
        return remote(part, part, sem, device)

    def some_half(buf, h, count, sem, device):
        part = buf.at[h, pl.ds(0, count)]
        return remote(part, part, sem, device)

    stores = []

    def store(src, dst):
        one = pltpu.make_async_copy(src, dst, osem.at[len(stores)])
        one.start()
        stores.append(one)

    def blocks_of(val):
        return [
            val[th * 128:(th + 1) * 128, h * 128:(h + 1) * 128].T for h in range(2) for th in range(2)
        ]

    def channels_of(blks):
        return jnp.concatenate(
            [jnp.concatenate([blks[2 * h], blks[2 * h + 1]], 1) for h in range(2)], 0
        )

    def tokens_of(blks):
        return jnp.concatenate(
            [jnp.concatenate([blks[th].T, blks[2 + th].T], 1) for th in range(2)], 0
        )

    def rotate(left, right):
        (lh, ll), (rh, rl) = split(left), split(right)
        return dot(jnp.concatenate([lh, rh, lh, rh, ll, rl], 1), b_ref[...])

    def forward(blks):
        sig = jnp.concatenate(blks, 1).astype(BF16)
        spec = dot(a_ref[...], jnp.concatenate([sig, sig], 0))
        re, im = spec[:128], spec[128:]
        t_re, t_im = tr_ref[...], ti_ref[...]
        top, bottom = [], []
        for h in range(2):
            u, w = re[:, h * 256:(h + 1) * 256], im[:, h * 256:(h + 1) * 256]
            top.append(u * t_re - w * t_im)
            bottom.append(u * t_im + w * t_re)
        full = rotate(jnp.concatenate(top, 0), jnp.concatenate(bottom, 0))
        return full[:, :256], full[:, 256:]

    def inverse(re, im):
        full = rotate(im, re)
        u, w = full[:, 256:], full[:, :256]
        t_re, t_im = tr_ref[...], ti_ref[...]
        top, bottom = [], []
        for h in range(2):
            ur, wi = u[h * 128:(h + 1) * 128], w[h * 128:(h + 1) * 128]
            top.append(ur * t_re + wi * t_im)
            bottom.append(wi * t_re - ur * t_im)
        both = jnp.concatenate([jnp.concatenate(top, 1), jnp.concatenate(bottom, 1)], 0)
        hi, lo = split(both)
        sig = dot(c_ref[...], jnp.concatenate([hi, hi, lo], 0))
        return [sig[:, r * 128:(r + 1) * 128] for r in range(4)]

    loads[0].wait()
    loads[1].wait()
    prod[...] = k_ref[...].astype(F32) * v_ref[...].astype(F32)
    interleave(blocks_of(prod[...]), i4, s0)
    loads[2].wait()
    interleave(blocks_of(taps_ref[...]), i4, s1)
    loads[3].wait()
    loads[4].wait()
    pl.semaphore_wait(bar, NCTX)
    g_send = remote(g_ref, gboth, 9, sibling)
    g_send.start()
    w_send = remote(w_ref.at[:, pl.ds(pl.multiple_of((1 - ch) * 256, 256), 256)], w_oth, 10, sibling)
    w_send.start()
    send_all(s0, r0, 0)
    send_all(s1, r1, 1)

    loads[5].wait()
    g_send.wait_recv()
    mine, other = g_ref[...], gboth[...]
    first = ch == 0
    gfull[:, :256] = jnp.where(first, mine.astype(F32), other.astype(F32)).astype(BF16)
    gfull[:, 256:] = jnp.where(first, other.astype(F32), mine.astype(F32)).astype(BF16)
    dgat[...] = dot(gfull[...], w_ref[...], (((1,), (1,)), ((), ())))
    dmix[...] = dgat[...] * q_ref[...].astype(F32)
    interleave(blocks_of(dmix[...]), i4, s2)
    loads[11].wait()
    base_t[...] = channels_of(blocks_of(skip_ref[...] * prod[...]))
    q_t[...] = channels_of(blocks_of(q_ref[...].astype(F32)))
    send_all(s2, r2, 2)

    sk[...] = jnp.sum(dmix[...] * prod[...], axis=0, keepdims=True)
    for to in plane_order:
        remote(sk, rsk1.at[plane], 5, at_plane(to)).start()
    for i in range(6, 11):
        loads[i].wait()

    wait_all(s0, r0, 0)
    re, im = forward(separate(r0, i4, 4))
    sig_re[...], sig_im[...] = re, im
    wait_all(s1, r1, 1)
    re, im = forward(separate(r1, i4, 4))
    tap_re[...], tap_im[...] = re, im
    re, im = sig_re[...], sig_im[...]
    conv = inverse(re * tap_re[...] - im * tap_im[...], re * tap_im[...] + im * tap_re[...])
    interleave(conv, i4, s3)
    send_all(s3, r3, 3)

    some(rsk1, 15, 5, at_plane(plane_order[0])).wait_recv()
    rsk1[plane] = sk[...]
    sk2[...] = jnp.sum(rsk1[...], axis=0)
    for to in z_order:
        remote(sk2, rsk2.at[z], 6, at_z(to)).start()

    wait_all(s2, r2, 2)
    re, im = forward(separate(r2, i4, 4))
    lag_p = inverse(re * tap_re[...] + im * tap_im[...], im * tap_re[...] - re * tap_im[...])
    lag_f = inverse(re * sig_re[...] + im * sig_im[...], im * sig_re[...] - re * sig_im[...])
    interleave(lag_p + lag_f, i8, s4)
    if LAG_CUTS[0]:
        send_all(s4, r4, 4, 0, LAG_CUTS[0])

    wait_all(s3, r3, 3)
    mixed_t = channels_of(separate(r3, i4, 4)) + base_t[...]
    gated_t = (q_t[...] * mixed_t).astype(BF16)
    for h in range(PARTS):
        if h % 2 == 0:
            full = dot(gated_t, gfull[:, h * WIDTH:(h + 2) * WIDTH])
        part = full[:, h % 2 * WIDTH:(h % 2 + 1) * WIDTH]
        g1[h] = part.reshape(16, 16, WIDTH).astype(BF16)
        for to in plane_order:
            remote(g1.at[h, to], rg.at[h, plane], SCATTER[h], at_plane(to)).start()
    gat_oth[0] = gated_t
    gat_send = remote(gat_oth.at[0], gat_oth.at[1], 11, sibling)
    gat_send.start()
    send_all(s4, r4, 4, LAG_CUTS[0], LAG_CUTS[1])
    mixed = tokens_of(
        [mixed_t[h * 128:(h + 1) * 128, th * 128:(th + 1) * 128] for h in range(2) for th in range(2)]
    )
    gq_ref[...] = (dgat[...] * mixed).astype(BF16)
    store(gq_ref, gq_hbm)
    w_send.wait_recv()
    w_mine = w_ref[:, pl.ds(pl.multiple_of(ch * 256, 256), 256)]
    turned = (((0,), (0,)), ((), ()))
    part = dot(gated_t, w_mine, turned)
    gat_send.wait_recv()
    out_ref[...] = (part + dot(gat_oth[1], w_oth[...], turned)).astype(BF16)
    store(out_ref, out_hbm)

    for h in range(PARTS):
        some_half(rg, h, 15, SCATTER[h], at_plane(plane_order[0])).wait_recv()
        rg[h, plane] = g1[h, plane]
        rz[h, z] = jnp.sum(rg[h].astype(F32), axis=0).astype(BF16)
        for to in z_order:
            remote(rz.at[h, z], rz.at[h, z], ACROSS[h], at_z(to)).start()
    send_all(s4, r4, 4, LAG_CUTS[1], NCTX - 1)
    some(rsk2, 7, 6, at_z(z_order[0])).wait_recv()
    rsk2[z] = sk2[...]
    gs_ref[...] = jnp.sum(rsk2[...], axis=0) / ROOT
    store(gs_ref, gs_hbm)
    for h in range(PARTS):
        some_half(rz, h, 7, ACROSS[h], at_z(z_order[0])).wait_recv()
        ga[h, plane] = (jnp.sum(rz[h].astype(F32), axis=0) / ROOT).astype(BF16)
        for to in plane_order:
            remote(ga.at[h, plane], ga.at[h, plane], GATHER[h], at_plane(to)).start()

    wait_all(s4, r4, 4)
    blks = separate(r4, i8, 8)
    grad_prod = tokens_of(blks[:4]) + skip_ref[...] * dmix[...]
    gk_ref[...] = (grad_prod * v_ref[...].astype(F32)).astype(BF16)
    gv_ref[...] = (grad_prod * k_ref[...].astype(F32)).astype(BF16)
    gf_ref[...] = tokens_of(blks[4:]).astype(BF16)
    store(gk_ref, gk_hbm)
    store(gv_ref, gv_hbm)
    store(gf_ref, gf_hbm)

    whole(s0, r0, 0).wait_send()
    whole(s1, r1, 1).wait_send()
    whole(s2, r2, 2).wait_send()
    whole(s3, r3, 3).wait_send()
    whole(s4, r4, 4).wait_send()
    some(rsk1, 15, 5, at_plane(plane_order[0])).wait_send()
    some(rsk2, 7, 6, at_z(z_order[0])).wait_send()
    for h in range(PARTS):
        some_half(rg, h, 15, SCATTER[h], at_plane(plane_order[0])).wait_send()
        some_half(rz, h, 7, ACROSS[h], at_z(z_order[0])).wait_send()
    g_send.wait_send()
    w_send.wait_send()
    gat_send.wait_send()

    for h in range(PARTS):
        last = some_half(ga, h, 15, GATHER[h], at_plane(plane_order[0]))
        last.wait_recv()
        store(ga.at[h], gw_hbm.at[h])
        last.wait_send()
    for one in stores:
        one.wait()


def finish(*refs):
    src, dst, mid, taps, wide, sem = refs[:7], refs[7:14], refs[14:21], refs[21], refs[22], refs[23]
    last = list(mid[:4]) + [taps, mid[5]]
    columns = [slice(h * WIDTH, (h + 1) * WIDTH) for h in range(PARTS)]
    loads = [pltpu.make_async_copy(src[i], mid[i], sem.at[0, i]) for i in range(6)]
    parts = [
        pltpu.make_async_copy(src[6].at[h], mid[6].at[h], sem.at[0, 6 + h]) for h in range(PARTS)
    ]
    stores = [pltpu.make_async_copy(last[i], dst[i], sem.at[1, i]) for i in range(6)]
    outs = [
        pltpu.make_async_copy(wide.at[:, columns[h]], dst[6].at[:, columns[h]], sem.at[1, 6 + h])
        for h in range(PARTS)
    ]
    for one in parts[:2] + [loads[4]] + parts[2:] + loads[:4] + [loads[5]]:
        one.start()
    for h in range(PARTS):
        parts[h].wait()
        wide[:, columns[h]] = mid[6][h].astype(F32).reshape(256, WIDTH)
        outs[h].start()
        if h == 1:
            loads[4].wait()
            taps[...] = mid[4][...].astype(F32) / ROOT
            stores[4].start()
    for i in (0, 1, 2, 3, 5):
        loads[i].wait()
        stores[i].start()
    for one in stores + outs:
        one.wait()


def shards(query_act, key_act, value_act, filter_taps, skip_gain, out_weight, out_grad):
    a_cat, b_cat, c_cat, t_re, t_im = (jnp.asarray(t) for t in tables())
    anywhere = pl.BlockSpec(memory_space=pl.ANY)
    sds = jax.ShapeDtypeStruct
    operands = (
        query_act, key_act, value_act, filter_taps, skip_gain[None, :], out_weight, out_grad,
        a_cat, b_cat, c_cat, t_re, t_im,
    )
    results = (
        sds((256, 256), BF16), sds((256, 256), BF16), sds((256, 256), BF16),
        sds((256, 256), BF16), sds((256, 256), F32), sds((1, 256), F32), sds((256, 512), F32),
    )
    msg4, msg8 = pltpu.VMEM((128, 4, 128), BF16), pltpu.VMEM((128, 8, 128), BF16)
    square, half = pltpu.VMEM((256, 256), F32), pltpu.VMEM((256, 256), BF16)
    halves = sds((PARTS, 16, 16, WIDTH), BF16)
    middle = results[:4] + (sds((256, 256), BF16), results[5], halves)
    outs = pl.pallas_call(
        kernel,
        out_shape=middle,
        in_specs=[anywhere] * 12,
        out_specs=[anywhere] * 7,
        scratch_shapes=[pltpu.VMEM(op.shape, op.dtype) for op in operands] + [
            msg4, msg4, msg4, msg4, msg4, msg4, msg4, msg4, msg8, msg8,
            pltpu.VMEM((1024, 128), F32), pltpu.VMEM((512, 128), F32),
            square, square, square, square, square,
            pltpu.VMEM((256, 512), BF16), half, half, pltpu.VMEM((2, 256, 256), BF16),
            square, square, square, square,
            pltpu.VMEM((PARTS, 16, 16, WIDTH), BF16), pltpu.VMEM((PARTS, 16, 16, WIDTH), BF16),
            pltpu.VMEM((PARTS, 8, 16, WIDTH), BF16), pltpu.VMEM((PARTS, 16, 16, WIDTH), BF16),
            pltpu.VMEM((1, 256), F32), pltpu.VMEM((16, 1, 256), F32),
            pltpu.VMEM((1, 256), F32), pltpu.VMEM((8, 1, 256), F32),
            half, half, half, half, half, pltpu.VMEM((1, 256), F32),
            pltpu.SemaphoreType.DMA((12,)), pltpu.SemaphoreType.DMA((12,)), pltpu.SemaphoreType.DMA((5,)),
            pltpu.SemaphoreType.DMA((22,)), pltpu.SemaphoreType.DMA((22,)),
        ],
        compiler_params=pltpu.CompilerParams(
            collective_id=0, has_side_effects=True, vmem_limit_bytes=56 * 1024 * 1024
        ),
        name="hyena",
    )(*operands)
    outs = pl.pallas_call(
        finish,
        out_shape=results,
        in_specs=[anywhere] * 7,
        out_specs=[anywhere] * 7,
        scratch_shapes=[pltpu.VMEM(res.shape, res.dtype) for res in middle]
        + [pltpu.VMEM((256, 256), F32), pltpu.VMEM((256, 512), F32), pltpu.SemaphoreType.DMA((2, 6 + PARTS))],
        name="finish",
    )(*outs)
    out, gq, gk, gv, gf, gs, gw = outs
    return out, gq, gk, gv, gf, gs.reshape(256), gw


def solution(mesh):
    spec = P("ctx", "ch")
    in_specs = (spec, spec, spec, spec, P("ch"), P("ch", None), spec)
    out_specs = (spec, spec, spec, spec, spec, P("ch"), P("ch", None))
    return jax.shard_map(shards, mesh=mesh, in_specs=in_specs, out_specs=out_specs, check_vma=False)
```
